32 devices in a mesh: dp: 4 (over x, core), seq: 2 (over y), mp: 4 (over z).
Axes of the slice: x: 2, y: 2, z: 4, core: 2. Of those that a mesh axis runs over, the one named last changes fastest.
Arguments:
- tokens: bfloat16 [8, 1024, 2048], P('dp', 'seq'), may hold values from -6 to 6
- block_ids: int32 [8, 1024], P('dp'), may hold values from 0 to 7, never falling along the last dimension, each value on 1 to 256 neighbouring positions
- query_weight: bfloat16 [2048, 2048], P(('dp', 'seq'), 'mp'), may hold values from -0.125 to 0.125
- key_weight: bfloat16 [2048, 2048], P(('dp', 'seq'), 'mp'), may hold values from -0.125 to 0.125
- value_weight: bfloat16 [2048, 2048], P(('dp', 'seq'), 'mp'), may hold values from -0.125 to 0.125
- out_weight: bfloat16 [2048, 2048], P(('dp', 'seq'), 'mp'), may hold values from -2 to 2
- gate_weight: bfloat16 [2048, 8192], P(('dp', 'seq'), 'mp'), may hold values from -0.125 to 0.125
- up_weight: bfloat16 [2048, 8192], P(('dp', 'seq'), 'mp'), may hold values from -0.125 to 0.125
- down_weight: bfloat16 [2048, 8192], P(('dp', 'seq'), 'mp'), may hold values from -0.0625 to 0.0625
- out_grad: bfloat16 [8, 1024, 2048], P('dp', 'seq'), may hold values from -6 to 6
Outputs:
- output: bfloat16 [8, 1024, 2048], P('dp', 'seq')
- tokens_grad: bfloat16 [8, 1024, 2048], P('dp', 'seq')
- query_grad: float32 [2048, 2048], P(('dp', 'seq'), 'mp')
- key_grad: float32 [2048, 2048], P(('dp', 'seq'), 'mp')
- value_grad: float32 [2048, 2048], P(('dp', 'seq'), 'mp')
- out_weight_grad: float32 [2048, 2048], P(('dp', 'seq'), 'mp')
- gate_grad: float32 [2048, 8192], P(('dp', 'seq'), 'mp')
- up_grad: float32 [2048, 8192], P(('dp', 'seq'), 'mp')
- down_grad: float32 [2048, 8192], P(('dp', 'seq'), 'mp')
The draws below stay inside these ranges and needn't reach their ends.
Inputs may be any that keep to these rules, and one draw needn't show every extreme that they name: `block_ids`: along each sequence the block numbers never fall; every number from 0 to 7 appears; a block holds 1 to 256 positions and some block holds exactly 256.
All inputs are finite; a program needn't handle non-finite values.
Results may differ from the reference program's by a relative error of at most 0.023.
Values may be sent and summed in bfloat16 or wider, within the bound.
A program may use at most 256 MiB of HBM per device.

```python
import math
import jax
import jax.numpy as jnp
import numpy as np
from jax import lax

D = 2048
HEADS = 16
HD = 128
FF = 8192
BLOCK = 256
LEN = 1024
SEQS = 8
SEGS = 8


def spiked(entries, stream_key, source, target, shards_of, factor):
    owner, partner = [(jnp.arange(entries.shape[axis_at]) // (entries.shape[axis_at] // shards_of)).reshape([-1 if axis == axis_at else 1 for axis in range(entries.ndim)]) for axis_at in (source, target)]
    chosen = jax.random.permutation(stream_key, shards_of)[partner]
    strong = (owner == chosen) | (owner == (partner + shards_of // 2) % shards_of)
    return jnp.where(strong, factor * entries, entries)


def block_levels(rng, dims, cuts, smallest, largest):
    loudness, own = 1.0, jax.random.fold_in(rng, 6)
    for axis_at, blocks in cuts:
        steps = jnp.exp(jax.random.uniform(jax.random.fold_in(own, axis_at), (blocks,), jnp.float32, smallest / len(cuts), largest / len(cuts)))
        loudness = loudness * jnp.repeat(steps, dims[axis_at] // blocks).reshape([-1 if axis == axis_at else 1 for axis in range(len(dims))])
    return loudness


def profile(amount, total, most, lean):
    portions = [(1 << 20) // math.isqrt(standing ** lean) + 1 for standing in range(2, amount + 1)]
    rest, given = total - most - (amount - 1), [1] * (amount - 1)
    while rest > 0:
        candidates = [i for i in range(amount - 1) if given[i] < most]
        pool, remaining = sum([portions[i] for i in candidates]), rest
        for i in candidates:
            extra = min(most - given[i], max(1, remaining * portions[i] // pool), rest)
            given[i] = given[i] + extra
            rest = rest - extra
    return np.array([most] + given)


def uneven(own_key, number_of, total, reach, slope):
    if number_of == 2:
        one = jax.random.randint(own_key, (), max(1, total - reach), min(reach, total - 1) + 1)
        return jnp.stack([one, total - one])
    sizes = jnp.asarray(profile(number_of, total, reach, slope), jnp.int32)
    pairs = (number_of - 1) // 2
    source_of, receiver = sizes[1:1 + 2 * pairs:2], sizes[2:2 + 2 * pairs:2]
    slack = jnp.minimum(source_of - 1, reach - receiver)
    moved = jax.random.randint(jax.random.fold_in(own_key, 1), (pairs,), 0, 1 << 20) % (slack + 1)
    sizes = sizes.at[1:1 + 2 * pairs:2].set(source_of - moved).at[2:2 + 2 * pairs:2].set(receiver + moved)
    return sizes[jax.random.permutation(jax.random.fold_in(own_key, 2), number_of)]


def bell_draw(stream_key, shape, width, most, shards=(), kind=jnp.bfloat16):
    values = jax.random.normal(stream_key, shape, jnp.float32) * width
    if len(shards) > 0:
        values = block_levels(stream_key, shape, shards, -0.22, 0.18) * values
    return jnp.clip(values, min=-most, max=most).astype(kind)


def gaussian_with(stream_key, extent, width, reach, shards, heavy, held_as=jnp.bfloat16):
    drawn = width * jax.random.normal(stream_key, extent, jnp.float32)
    if shards:
        drawn = drawn * block_levels(stream_key, extent, shards, -0.22, 0.18)
    return jnp.clip(spiked(drawn, jax.random.fold_in(stream_key, 3), *heavy), -reach, reach).astype(held_as)


def setup_inputs(seed: int = 0) -> dict:
    key_of = jax.random.split(jax.random.key(seed), 11)
    return {
        "tokens": bell_draw(key_of[0], (SEQS, LEN, D), 1.0, 6.0, ((0, 4), (1, 2))),
        "block_ids": jax.vmap(lambda own: jnp.searchsorted(jnp.cumsum(uneven(own, SEGS, LEN, BLOCK, 1)), jnp.arange(LEN), side="right"))(jax.random.split(key_of[1], SEQS)).reshape((SEQS, LEN)).astype(jnp.int32),
        "query_weight": bell_draw(key_of[2], (D, D), D ** -0.5, 0.125, ((0, 8), (1, 4))),
        "key_weight": bell_draw(key_of[3], (D, D), D ** -0.5, 0.125, ((0, 8), (1, 4))),
        "value_weight": bell_draw(key_of[4], (D, D), D ** -0.5, 0.125, ((0, 8), (1, 4))),
        "out_weight": bell_draw(key_of[5], (D, D), (max(4 * D // LEN, 1)) ** -0.5, 2.0, ((0, 8), (1, 4))),
        "gate_weight": bell_draw(key_of[6], (D, FF), D ** -0.5, 0.125, ((0, 8), (1, 4))),
        "up_weight": bell_draw(key_of[7], (D, FF), D ** -0.5, 0.125, ((0, 8), (1, 4))),
        "down_weight": bell_draw(key_of[8], (D, FF), FF ** -0.5, 0.0625, ((0, 8), (1, 4))),
        "out_grad": gaussian_with(key_of[9], (SEQS, LEN, D), 1.0, 6.0, ((0, 4), (1, 2)), (1, 2, 2, 2.0)),
    }


@jax.custom_vjp
def low(v):
    return lax.optimization_barrier(v.astype(jnp.bfloat16)).astype(jnp.float32)

@jax.custom_vjp
def low_back(v):
    return v

def low_keep(v):
    return (low(v), None)

def low_pass(kept, grad):
    return (grad,)

def back_keep(v):
    return (v, None)

def back_low(kept, grad):
    return (low(grad),)
low.defvjp(low_keep, low_pass)
low_back.defvjp(back_keep, back_low)
EPSILON = 1e-05
THETA = 10000.0
MASKED = -1e+30
HIGHEST = lax.Precision.HIGHEST

def product(first_arg, second_arg):
    return jnp.dot(first_arg, second_arg, precision=HIGHEST, preferred_element_type=jnp.float32)

def layer_norm(values):
    centered = values - lax.optimization_barrier(jnp.mean(values, axis=-1, keepdims=True))
    return centered * lax.rsqrt(lax.optimization_barrier(jnp.mean(centered * centered, axis=-1, keepdims=True)) + EPSILON)

def rope_tables(positions):
    steps_index = jnp.arange(HD // 2).astype(jnp.float32)
    frequency = jnp.exp(steps_index * (-2.0 * math.log(THETA) / HD))
    angles = positions[:, None] * frequency[None, :]
    cosine = jnp.concatenate([jnp.cos(angles), jnp.cos(angles)], axis=-1)
    sine_table = jnp.concatenate([jnp.sin(angles), jnp.sin(angles)], axis=-1)
    return (cosine, sine_table)

def rotate(values, cosine, sine_table):
    halfway = values.shape[-1] // 2
    turned = jnp.concatenate([-values[..., halfway:], values[..., :halfway]], axis=-1)
    return values * cosine + turned * sine_table

def attend(queries, keys, values, seq_ids):
    block_rows = min(512, LEN)

    def attend_block(block_index):
        offset = block_index * block_rows
        query_block = lax.dynamic_slice_in_dim(queries, offset, block_rows, 0)
        query_ids = lax.dynamic_slice_in_dim(seq_ids, offset, block_rows, 0)
        raw_scores = low_back(jnp.einsum('qhd,khd->hqk', query_block, keys, precision=HIGHEST))
        allowed = seq_ids[None, None, :] <= query_ids[None, :, None]
        scores = jnp.where(allowed, raw_scores / math.sqrt(HD), MASKED)
        weights = low(jax.nn.softmax(scores, axis=-1))
        mixed = jnp.einsum('hqk,khd->qhd', weights, values, precision=HIGHEST)
        return mixed.reshape(block_rows, HEADS * HD)
    pieces = lax.map(jax.checkpoint(attend_block), jnp.arange(LEN // block_rows, dtype=jnp.int32))
    return pieces.reshape(LEN, HEADS * HD)

def forward(inputs, seq_ids, cosine, sine_table, query_weight, key_weight, value_weight, out_weight, gate_weight, up_weight, down_weight):
    heads_shape = (LEN, HEADS, HD)
    normed = low(layer_norm(inputs))
    queries = low(rotate(low_back(product(normed, query_weight)).reshape(heads_shape), cosine, sine_table))
    keys = low(rotate(low_back(product(normed, key_weight)).reshape(heads_shape), cosine, sine_table))
    values = low(low_back(product(normed, value_weight))).reshape(heads_shape)
    attended = low(low_back(attend(queries, keys, values, seq_ids)))
    middle = inputs + low_back(product(attended, out_weight.T))
    normed_two = low(layer_norm(middle))
    gate_values = low_back(product(normed_two, gate_weight))
    up_values = low_back(product(normed_two, up_weight))
    hidden = low(jax.nn.silu(gate_values) * up_values)
    return middle + low_back(product(hidden, down_weight.T))

def reference(tokens, block_ids, query_weight, key_weight, value_weight, out_weight, gate_weight, up_weight, down_weight, out_grad):
    weights = tuple((weight.astype(jnp.float32) for weight in (query_weight, key_weight, value_weight, out_weight, gate_weight, up_weight, down_weight)))
    positions = jnp.arange(LEN).astype(jnp.float32)
    cosine, sine_table = rope_tables(positions)
    cosine = cosine[:, None, :]
    sine_table = sine_table[:, None, :]

    def per_sequence(totals, sequence_item):
        seq_tokens, seq_ids, seq_grad = sequence_item

        def run_layer(inputs, *layer_weights):
            return forward(inputs, seq_ids, cosine, sine_table, *layer_weights)
        result, pullback = jax.vjp(run_layer, seq_tokens.astype(jnp.float32), *weights)
        gradients = pullback(seq_grad.astype(jnp.float32))
        totals = tuple((running + grad_part for running, grad_part in zip(totals, gradients[1:])))
        return (totals, (result.astype(jnp.bfloat16), gradients[0].astype(jnp.bfloat16)))
    zero_grads = tuple((jnp.zeros_like(weight) for weight in weights))
    totals, (outputs, input_grads) = lax.scan(per_sequence, zero_grads, (tokens, block_ids, out_grad))
    return (outputs, input_grads, totals[0], totals[1], totals[2], totals[3], totals[4], totals[5], totals[6])
```

```python
import functools
import math

import jax
import jax.numpy as jnp
from jax import lax
from jax.experimental import pallas as pl
from jax.experimental.pallas import tpu as pltpu
from jax.sharding import PartitionSpec as P

HD = 128


EPSILON = 1e-05
THETA = 10000.0
MASKED = -1e30


def layer_norm(values):
    centered = values - jnp.mean(values, axis=-1, keepdims=True)
    inverse = lax.rsqrt(jnp.mean(centered * centered, axis=-1, keepdims=True) + EPSILON)
    return (centered * inverse, inverse)


def norm_back(normed, inverse, upstream):
    middle_term = upstream - jnp.mean(upstream, axis=-1, keepdims=True)
    return inverse * (middle_term - normed * jnp.mean(upstream * normed, axis=-1, keepdims=True))


def rope_tables(positions):
    steps_index = jnp.arange(HD // 2).astype(jnp.float32)
    frequency = jnp.exp(steps_index * (-2.0 * math.log(THETA) / HD))
    angles = positions[:, None] * frequency[None, :]
    cosine = jnp.concatenate([jnp.cos(angles), jnp.cos(angles)], axis=-1)
    sine_table = jnp.concatenate([jnp.sin(angles), jnp.sin(angles)], axis=-1)
    return (cosine, sine_table)


def rotate(values, cosine, sine_table):
    halfway = values.shape[-1] // 2
    turned = jnp.concatenate([-values[..., halfway:], values[..., :halfway]], axis=-1)
    return values * cosine + turned * sine_table


def unrotate(values, cosine, sine_table):
    halfway = values.shape[-1] // 2
    scaled = values * sine_table
    turned = jnp.concatenate([scaled[..., halfway:], -scaled[..., :halfway]], axis=-1)
    return values * cosine + turned


def matmul(factor_left, factor_right):
    return jnp.dot(factor_left, factor_right, preferred_element_type=jnp.float32)


def matmul_trans(factor_left, factor_right):
    return lax.dot_general(
        factor_left, factor_right, (((1,), (1,)), ((), ())), preferred_element_type=jnp.float32
    )


def outer_sum(factor_left, factor_right):
    return lax.dot_general(
        factor_left, factor_right, (((0,), (0,)), ((), ())), preferred_element_type=jnp.float32
    )


def general_body(
    tokens,
    block_ids,
    query_weight,
    key_weight,
    value_weight,
    out_weight,
    gate_weight,
    up_weight,
    down_weight,
    out_grad,
):
    groups, shard_len, model_width = tokens.shape
    seq_rank = lax.axis_index("seq")
    seq_len = shard_len * lax.axis_size("seq")
    row_count = groups * shard_len
    shards = (
        query_weight,
        key_weight,
        value_weight,
        out_weight,
        gate_weight,
        up_weight,
        down_weight,
    )
    full_query, full_key, full_value, full_out, full_gate, full_up, full_down = (
        lax.all_gather(shards[0], ("dp", "seq"), axis=0, tiled=True),
        lax.all_gather(shards[1], ("dp", "seq"), axis=0, tiled=True),
        lax.all_gather(shards[2], ("dp", "seq"), axis=0, tiled=True),
        lax.all_gather(shards[3], ("dp", "seq"), axis=0, tiled=True),
        lax.all_gather(shards[4], ("dp", "seq"), axis=0, tiled=True),
        lax.all_gather(shards[5], ("dp", "seq"), axis=0, tiled=True),
        lax.all_gather(shards[6], ("dp", "seq"), axis=0, tiled=True),
    )
    heads_here = full_query.shape[1] // HD
    shape_heads = (groups, shard_len, heads_here, HD)
    score_root = math.sqrt(HD)
    positions = (seq_rank * shard_len + jnp.arange(shard_len)).astype(jnp.float32)
    cosine, sine_table = rope_tables(positions)
    cosine = cosine[None, :, None, :]
    sine_table = sine_table[None, :, None, :]
    inputs = tokens.astype(jnp.float32).reshape(row_count, model_width)
    normed, inverse = layer_norm(inputs)
    normed_low = normed.astype(jnp.bfloat16)
    queries = rotate(
        matmul(normed_low, full_query).reshape(shape_heads), cosine, sine_table
    ).astype(jnp.bfloat16)
    key_local = (
        rotate(matmul(normed_low, full_key).reshape(shape_heads), cosine, sine_table)
        .astype(jnp.bfloat16)
        .reshape(groups, shard_len, -1)
    )
    value_local = matmul(normed_low, full_value).astype(jnp.bfloat16).reshape(groups, shard_len, -1)
    keys_all, values_all = (
        lax.all_gather(key_local, "seq", axis=1, tiled=True),
        lax.all_gather(value_local, "seq", axis=1, tiled=True),
    )
    query_ids = lax.dynamic_slice_in_dim(block_ids, seq_rank * shard_len, shard_len, 1)
    last_ids = query_ids[:, shard_len - 1 :]
    reached = jnp.sum((block_ids <= last_ids).astype(jnp.int32), axis=1)
    key_blocks = (jnp.max(reached) + shard_len - 1) // shard_len

    def block_scores(keys_source, offset):
        key_block = lax.dynamic_slice_in_dim(keys_source, offset, shard_len, 1).reshape(shape_heads)
        raw_scores = jnp.einsum(
            "gqhd,gkhd->ghqk", queries, key_block, preferred_element_type=jnp.float32
        )
        key_ids = lax.dynamic_slice_in_dim(block_ids, offset, shard_len, 1)
        allowed = key_ids[:, None, None, :] <= query_ids[:, None, :, None]
        return (jnp.where(allowed, raw_scores / score_root, MASKED), allowed, key_block)

    def stats_step(block_index, loop_state):
        running_max, running_sum = loop_state
        scores, allowed, key_block = block_scores(keys_all, block_index * shard_len)
        new_max = jnp.maximum(running_max, jnp.max(scores, axis=-1))
        weights_block = jnp.where(allowed, jnp.exp(scores - new_max[..., None]), 0.0)
        return (
            new_max,
            running_sum * jnp.exp(running_max - new_max) + jnp.sum(weights_block, axis=-1),
        )

    stat_shape = (groups, heads_here, shard_len)
    running_max, running_sum = lax.fori_loop(
        0,
        key_blocks,
        stats_step,
        (jnp.full(stat_shape, MASKED, jnp.float32), jnp.zeros(stat_shape, jnp.float32)),
    )
    log_total = running_max + jnp.log(running_sum)

    def output_step(block_index, accumulated):
        offset = block_index * shard_len
        scores, allowed, key_block = block_scores(keys_all, offset)
        weights_block = jnp.where(allowed, jnp.exp(scores - log_total[..., None]), 0.0).astype(
            jnp.bfloat16
        )
        value_block = lax.dynamic_slice_in_dim(values_all, offset, shard_len, 1).reshape(
            shape_heads
        )
        return accumulated + jnp.einsum(
            "ghqk,gkhd->gqhd", weights_block, value_block, preferred_element_type=jnp.float32
        )

    attended = lax.fori_loop(0, key_blocks, output_step, jnp.zeros(shape_heads, jnp.float32))
    attended_low = attended.astype(jnp.bfloat16).reshape(row_count, -1)
    branch = lax.psum(matmul_trans(attended_low, full_out).astype(jnp.bfloat16), "mp").astype(
        jnp.float32
    )
    middle = inputs + branch
    normed_two, inverse_two = layer_norm(middle)
    normed_two_low = normed_two.astype(jnp.bfloat16)
    gate_values = matmul(normed_two_low, full_gate)
    up_values = matmul(normed_two_low, full_up)
    sigmoid_gate = jax.nn.sigmoid(gate_values)
    activated = gate_values * sigmoid_gate
    hidden_low = (activated * up_values).astype(jnp.bfloat16)
    feed_out = lax.psum(matmul_trans(hidden_low, full_down).astype(jnp.bfloat16), "mp").astype(
        jnp.float32
    )
    output = (middle + feed_out).astype(jnp.bfloat16).reshape(groups, shard_len, model_width)
    full_query, full_key, full_value, full_out, full_gate, full_up, full_down = (
        lax.all_gather(shards[0], ("dp", "seq"), axis=0, tiled=True),
        lax.all_gather(shards[1], ("dp", "seq"), axis=0, tiled=True),
        lax.all_gather(shards[2], ("dp", "seq"), axis=0, tiled=True),
        lax.all_gather(shards[3], ("dp", "seq"), axis=0, tiled=True),
        lax.all_gather(shards[4], ("dp", "seq"), axis=0, tiled=True),
        lax.all_gather(shards[5], ("dp", "seq"), axis=0, tiled=True),
        lax.all_gather(shards[6], ("dp", "seq"), axis=0, tiled=True),
    )
    grad_low = out_grad.reshape(row_count, model_width)
    down_term = outer_sum(grad_low, hidden_low)
    grad_hidden = matmul(grad_low, full_down)
    grad_gate = (
        grad_hidden * up_values * sigmoid_gate * (1.0 + gate_values * (1.0 - sigmoid_gate))
    ).astype(jnp.bfloat16)
    grad_up = (grad_hidden * activated).astype(jnp.bfloat16)
    gate_term = outer_sum(normed_two_low, grad_gate)
    up_term = outer_sum(normed_two_low, grad_up)
    grad_normed_two = lax.psum(
        (matmul_trans(grad_gate, full_gate) + matmul_trans(grad_up, full_up)).astype(jnp.bfloat16),
        "mp",
    ).astype(jnp.float32)
    grad_middle = grad_low.astype(jnp.float32) + norm_back(normed_two, inverse_two, grad_normed_two)
    grad_branch = grad_middle.astype(jnp.bfloat16)
    out_term = outer_sum(grad_branch, attended_low)
    grad_attended = matmul(grad_branch, full_out).astype(jnp.bfloat16).reshape(shape_heads)
    row_delta = jnp.einsum("gqhd,gqhd->ghq", grad_attended.astype(jnp.float32), attended)

    def backward_step(block_index, loop_state):
        grad_queries, grad_keys, grad_values = loop_state
        offset = block_index * shard_len
        scores, allowed, key_block = block_scores(keys_all, offset)
        weights_block = jnp.where(allowed, jnp.exp(scores - log_total[..., None]), 0.0)
        value_block = lax.dynamic_slice_in_dim(values_all, offset, shard_len, 1).reshape(
            shape_heads
        )
        grad_weights = jnp.einsum(
            "gqhd,gkhd->ghqk", grad_attended, value_block, preferred_element_type=jnp.float32
        )
        grad_raw = (weights_block * (grad_weights - row_delta[..., None]) / score_root).astype(
            jnp.bfloat16
        )
        grad_queries = grad_queries + jnp.einsum(
            "ghqk,gkhd->gqhd", grad_raw, key_block, preferred_element_type=jnp.float32
        )
        key_part = jnp.einsum(
            "ghqk,gqhd->gkhd", grad_raw, queries, preferred_element_type=jnp.float32
        ).reshape(groups, shard_len, -1)
        value_part = jnp.einsum(
            "ghqk,gqhd->gkhd",
            weights_block.astype(jnp.bfloat16),
            grad_attended,
            preferred_element_type=jnp.float32,
        ).reshape(groups, shard_len, -1)
        grad_keys = lax.dynamic_update_slice_in_dim(grad_keys, key_part, offset, 1)
        grad_values = lax.dynamic_update_slice_in_dim(grad_values, value_part, offset, 1)
        return (grad_queries, grad_keys, grad_values)

    zero_full = jnp.zeros((groups, seq_len, heads_here * HD), jnp.float32)
    grad_queries, grad_keys, grad_values = lax.fori_loop(
        0, key_blocks, backward_step, (jnp.zeros(shape_heads, jnp.float32), zero_full, zero_full)
    )
    grad_key_sum, grad_value_sum = (
        lax.psum_scatter(
            grad_keys.astype(jnp.bfloat16), "seq", scatter_dimension=1, tiled=True
        ).astype(jnp.float32),
        lax.psum_scatter(
            grad_values.astype(jnp.bfloat16), "seq", scatter_dimension=1, tiled=True
        ).astype(jnp.float32),
    )
    grad_q_lin = (
        unrotate(grad_queries, cosine, sine_table).astype(jnp.bfloat16).reshape(row_count, -1)
    )
    grad_k_lin = (
        unrotate(grad_key_sum.reshape(shape_heads), cosine, sine_table)
        .astype(jnp.bfloat16)
        .reshape(row_count, -1)
    )
    grad_v_lin = grad_value_sum.astype(jnp.bfloat16).reshape(row_count, -1)
    query_term = outer_sum(normed_low, grad_q_lin)
    key_term = outer_sum(normed_low, grad_k_lin)
    value_term = outer_sum(normed_low, grad_v_lin)
    grad_partial = (
        matmul_trans(grad_q_lin, full_query)
        + matmul_trans(grad_k_lin, full_key)
        + matmul_trans(grad_v_lin, full_value)
    )
    grad_normed = lax.psum(grad_partial.astype(jnp.bfloat16), "mp").astype(jnp.float32)
    tokens_grad = (
        (grad_middle + norm_back(normed, inverse, grad_normed))
        .astype(jnp.bfloat16)
        .reshape(groups, shard_len, model_width)
    )
    grad_terms = (query_term, key_term, value_term, out_term, gate_term, up_term, down_term)
    query_grad, key_grad, value_grad, out_weight_grad, gate_grad, up_grad, down_grad = (
        lax.psum_scatter(
            grad_terms[0].astype(jnp.bfloat16), ("dp", "seq"), scatter_dimension=0, tiled=True
        ).astype(jnp.float32),
        lax.psum_scatter(
            grad_terms[1].astype(jnp.bfloat16), ("dp", "seq"), scatter_dimension=0, tiled=True
        ).astype(jnp.float32),
        lax.psum_scatter(
            grad_terms[2].astype(jnp.bfloat16), ("dp", "seq"), scatter_dimension=0, tiled=True
        ).astype(jnp.float32),
        lax.psum_scatter(
            grad_terms[3].astype(jnp.bfloat16), ("dp", "seq"), scatter_dimension=0, tiled=True
        ).astype(jnp.float32),
        lax.psum_scatter(
            grad_terms[4].astype(jnp.bfloat16), ("dp", "seq"), scatter_dimension=0, tiled=True
        ).astype(jnp.float32),
        lax.psum_scatter(
            grad_terms[5].astype(jnp.bfloat16), ("dp", "seq"), scatter_dimension=0, tiled=True
        ).astype(jnp.float32),
        lax.psum_scatter(
            grad_terms[6].astype(jnp.bfloat16), ("dp", "seq"), scatter_dimension=0, tiled=True
        ).astype(jnp.float32),
    )
    return (
        output,
        tokens_grad,
        query_grad,
        key_grad,
        value_grad,
        out_weight_grad,
        gate_grad,
        up_grad,
        down_grad,
    )


MESH = pl.DeviceIdType.MESH
ANY = pl.BlockSpec(memory_space=pl.ANY)
VMEM = pl.BlockSpec(memory_space=pltpu.VMEM)
BF = jnp.bfloat16
F32 = jnp.float32
VMEM_LIMIT = 60 * 1024 * 1024
CHUNK = 64
BLOCK_ROWS = 256
TILE = 256


def params(collective_id=None):
    if collective_id is None:
        return pltpu.CompilerParams(vmem_limit_bytes=VMEM_LIMIT)
    return pltpu.CompilerParams(
        collective_id=collective_id, has_side_effects=True, vmem_limit_bytes=VMEM_LIMIT
    )


def dot_nt(left, right):
    return lax.dot_general(left, right, (((1,), (1,)), ((), ())), preferred_element_type=F32)


def dot_tn(left, right):
    return lax.dot_general(left, right, (((0,), (0,)), ((), ())), preferred_element_type=F32)


def dot_nn(left, right):
    return jnp.dot(left, right, preferred_element_type=F32)


def rows_of(index, size):
    return pl.ds(pl.multiple_of(index * size, size), size)


def norm_parts(values):
    centered = values - jnp.mean(values, axis=-1, keepdims=True)
    inverse = lax.rsqrt(jnp.mean(centered * centered, axis=-1, keepdims=True) + EPSILON)
    return centered * inverse, inverse


class Tree:
    def __init__(self, count, acc, from_end, from_mid, out, sems):
        self.count, self.acc, self.from_end, self.from_mid, self.out = count, acc, from_end, from_mid, out
        self.sent, self.got_end, self.got_mid, self.fin_sent, self.fin_got, self.fin_kept = sems
        position = lax.axis_index("mp")
        self.outer = position + 1 - 2 * (position % 2)
        self.peer = 3 - position
        self.is_mid = (position + 1) // 2 == 1
        self.is_end = (position + 1) // 2 != 1

    def barrier(self, beside_seq=False):
        barrier = pltpu.get_barrier_semaphore()
        pl.semaphore_signal(barrier, inc=1, device_id={"mp": self.outer}, device_id_type=MESH)

        @pl.when(self.is_mid)
        def _():
            pl.semaphore_signal(barrier, inc=1, device_id={"mp": self.peer}, device_id_type=MESH)

        if beside_seq:
            other = 1 - lax.axis_index("seq")
            pl.semaphore_signal(barrier, inc=1, device_id={"seq": other}, device_id_type=MESH)
        extra = 2 if beside_seq else 1
        position = lax.axis_index("mp")
        pl.semaphore_wait(barrier, extra + (position * (3 - position)) // 2)

    def part(self, j):
        where = rows_of(j, CHUNK)
        return pltpu.make_async_remote_copy(
            self.acc.at[where], self.from_end.at[where], self.sent.at[j], self.got_end.at[j],
            device_id={"mp": self.outer}, device_id_type=MESH,
        )

    def pair(self, j):
        where = rows_of(j, CHUNK)
        return pltpu.make_async_remote_copy(
            self.acc.at[where], self.from_mid.at[where], self.sent.at[j], self.got_mid.at[j],
            device_id={"mp": self.peer}, device_id_type=MESH,
        )

    def final(self, j):
        where = rows_of(j, CHUNK)
        return pltpu.make_async_remote_copy(
            self.from_end.at[where], self.out.at[where], self.fin_sent.at[j], self.fin_got.at[j],
            device_id={"mp": self.outer}, device_id_type=MESH,
        )

    def keep(self, j):
        where = rows_of(j, CHUNK)
        return pltpu.make_async_copy(self.from_end.at[where], self.out.at[where], self.fin_kept.at[j])

    def send_block(self, block):
        per_block = BLOCK_ROWS // CHUNK

        @pl.when(self.is_end)
        def _():
            for s in range(per_block):
                self.part(block * per_block + s).start()

    def middle_step(self, i, lag_sum, lag_final, epilogue):
        j = i - lag_sum

        @pl.when(self.is_mid & (j >= 0) & (j < self.count))
        def _():
            self.part(j).wait_recv()
            where = rows_of(j, CHUNK)
            self.acc[where] = (self.acc[where].astype(F32) + self.from_end[where].astype(F32)).astype(BF)
            self.pair(j).start()

        k = i - lag_final

        @pl.when(self.is_mid & (k >= 0) & (k < self.count))
        def _():
            self.pair(k).wait_recv()
            where = rows_of(k, CHUNK)
            total = self.acc[where].astype(F32) + self.from_mid[where].astype(F32)
            self.from_end[where] = epilogue(k, total)
            self.final(k).start()
            self.keep(k).start()

    def drain(self):
        @pl.when(self.is_end)
        def _():
            def one(j, carry):
                self.part(j).wait_send()
                self.final(j).wait_recv()
                return carry

            lax.fori_loop(0, self.count, one, 0)

        @pl.when(self.is_mid)
        def _():
            def one(j, carry):
                self.pair(j).wait_send()
                self.final(j).wait_send()
                self.keep(j).wait()
                return carry

            lax.fori_loop(0, self.count, one, 0)


class Feed:
    def __init__(self, count, source, slots, sem):
        self.count, self.source, self.slots, self.sem = count, source, slots, sem

    def copy(self, j):
        return pltpu.make_async_copy(
            self.source.at[rows_of(j, CHUNK)], self.slots.at[j % 2], self.sem.at[j % 2]
        )

    def begin(self):
        self.copy(0).start()
        self.copy(1).start()

    def take(self, j):
        self.copy(j).wait()
        return self.slots[j % 2]

    def following(self, j):
        @pl.when(j + 2 < self.count)
        def _():
            self.copy(j + 2).start()


class Drop:
    def __init__(self, count, target, slots, sem):
        self.count, self.target, self.slots, self.sem = count, target, slots, sem

    def copy(self, j):
        return pltpu.make_async_copy(
            self.slots.at[j % 2], self.target.at[rows_of(j, CHUNK)], self.sem.at[j % 2]
        )

    def put(self, j, values):
        @pl.when(j >= 2)
        def _():
            self.copy(j - 2).wait()

        self.slots[j % 2] = values
        self.copy(j).start()

    def finish(self):
        self.copy(self.count - 2).wait()
        self.copy(self.count - 1).wait()


def tree_scratch(rows, width):
    count = rows // CHUNK
    buffers = [pltpu.VMEM((rows, width), BF) for _ in range(3)]
    return buffers + [pltpu.SemaphoreType.DMA((count,)) for _ in range(6)]


def attention_kernel(q_ref, k_ref, v_ref, ko_ref, vo_ref, qid_ref, kid_ref, koid_ref, o_ref, lse_ref):
    root = 1.0 / math.sqrt(HD)
    queries = q_ref[...]

    def scores(keys, ids):
        raw = dot_nt(keys, queries) * root
        return jnp.where(ids <= qid_ref[0], raw, MASKED)

    own = scores(k_ref[...], kid_ref[0])
    other = scores(ko_ref[...], koid_ref[0])
    top = jnp.maximum(jnp.max(own, axis=0, keepdims=True), jnp.max(other, axis=0, keepdims=True))
    own, other = jnp.exp(own - top), jnp.exp(other - top)
    total = jnp.sum(own, axis=0, keepdims=True) + jnp.sum(other, axis=0, keepdims=True)
    scale = 1.0 / total
    mixed = dot_tn(v_ref[...], (own * scale).astype(BF)) + dot_tn(vo_ref[...], (other * scale).astype(BF))
    o_ref[...] = mixed.T.astype(BF)
    lse_ref[0] = top + jnp.log(total)


def attention(queries, kv_own, kv_other, qid, kid, koid, groups, shard_len):
    rows, width = queries.shape
    heads = width // HD
    tile = lambda shift: pl.BlockSpec((shard_len, HD), lambda g, h: (g, h + shift))
    row = pl.BlockSpec((1, 1, shard_len), lambda g, h: (g, 0, 0))
    column = pl.BlockSpec((1, shard_len, 1), lambda g, h: (g, 0, 0))
    return pl.pallas_call(
        attention_kernel,
        grid=(groups, heads),
        out_shape=(
            jax.ShapeDtypeStruct((rows, width), BF),
            jax.ShapeDtypeStruct((groups * heads, 1, shard_len), F32),
        ),
        in_specs=[tile(0), tile(0), tile(heads), tile(0), tile(heads), row, column, column],
        out_specs=(tile(0), pl.BlockSpec((1, 1, shard_len), lambda g, h: (g * heads + h, 0, 0))),
        compiler_params=params(),
    )(queries, kv_own, kv_own, kv_other, kv_other, qid, kid, koid)


def branch_kernel(count, att_ref, w_ref, tok_ref, n2_ref, mid_ref, acc, from_end, from_mid, *rest):
    sems, (mid_slots, mid_sem) = rest[:6], rest[6:]
    tree = Tree(count, acc, from_end, from_mid, n2_ref, sems)
    drop = Drop(count, mid_ref, mid_slots, mid_sem)
    tree.barrier()
    per_block = BLOCK_ROWS // CHUNK

    def epilogue(j, total):
        middle = tok_ref[rows_of(j, CHUNK)].astype(F32) + total
        drop.put(j, middle)
        return norm_parts(middle)[0].astype(BF)

    def step(i, carry):
        @pl.when((i % per_block == 0) & (i < count))
        def _():
            block = i // per_block
            where = rows_of(block, BLOCK_ROWS)
            acc[where] = dot_nt(att_ref[where], w_ref[...]).astype(BF)
            tree.send_block(block)

        tree.middle_step(i, 1, 3, epilogue)
        return carry

    lax.fori_loop(0, count + 3, step, 0)
    tree.drain()

    @pl.when(tree.is_mid)
    def _():
        drop.finish()


def branch_sum(attended, merged, tokens):
    rows, width = attended.shape
    model = tokens.shape[1]
    count = rows // CHUNK
    return pl.pallas_call(
        functools.partial(branch_kernel, count),
        grid=(1,),
        out_shape=(jax.ShapeDtypeStruct((rows, model), BF), jax.ShapeDtypeStruct((rows, model), F32)),
        in_specs=[VMEM, pl.BlockSpec((model, width), lambda _: (0, 3)), VMEM],
        out_specs=(ANY, ANY),
        scratch_shapes=tree_scratch(rows, model)
        + [pltpu.VMEM((2, CHUNK, model), F32), pltpu.SemaphoreType.DMA((2,))],
        compiler_params=params(1),
    )(attended, merged, tokens)


def feed_kernel(
    count, n2_ref, og_ref, wf_ref, mid_ref, gb_ref, gm_ref, hid_ref, ggu_ref,
    acc, from_end, from_mid, *rest,
):
    sems, rest = rest[:6], rest[6:]
    wg, wu, wd, w_sem, xs, ogs, in_sem, hs, gs, us, out_sem, mid_slots, mid_sem, og_slots, og_sem, gm_slots, gm_sem = rest
    tree = Tree(count, acc, from_end, from_mid, gb_ref, sems)
    mid_feed = Feed(count, mid_ref, mid_slots, mid_sem)
    og_feed = Feed(count, og_ref, og_slots, og_sem)
    drop = Drop(count, gm_ref, gm_slots, gm_sem)
    hidden = wg.shape[1]
    per_block = BLOCK_ROWS // CHUNK
    blocks = count // per_block

    def weight(k, target):
        return pltpu.make_async_copy(wf_ref.at[:, pl.ds(k * hidden, hidden)], target, w_sem.at[k])

    def load(block):
        where, slot = rows_of(block, BLOCK_ROWS), block % 2
        return (
            pltpu.make_async_copy(n2_ref.at[where], xs.at[slot], in_sem.at[0, slot]),
            pltpu.make_async_copy(og_ref.at[where], ogs.at[slot], in_sem.at[1, slot]),
        )

    def store(block):
        where = rows_of(block, BLOCK_ROWS)
        return (
            pltpu.make_async_copy(hs, hid_ref.at[where], out_sem.at[0]),
            pltpu.make_async_copy(gs, ggu_ref.at[where, pl.ds(0, hidden)], out_sem.at[1]),
            pltpu.make_async_copy(us, ggu_ref.at[where, pl.ds(hidden, hidden)], out_sem.at[2]),
        )

    for block in range(2):
        for copy in load(block):
            copy.start()
    for k, target in enumerate((wg, wu, wd)):
        weight(k, target).start()

    @pl.when(tree.is_mid)
    def _():
        mid_feed.begin()
        og_feed.begin()

    tree.barrier()
    for k, target in enumerate((wg, wu, wd)):
        weight(k, target).wait()

    def epilogue(j, total):
        normed, inverse = norm_parts(mid_feed.take(j))
        og = og_feed.take(j).astype(F32)
        spread = total - jnp.mean(total, axis=-1, keepdims=True)
        grad = og + inverse * (spread - normed * jnp.mean(total * normed, axis=-1, keepdims=True))
        mid_feed.following(j)
        og_feed.following(j)
        drop.put(j, grad)
        return grad.astype(BF)

    def step(i, carry):
        block, quarter = i // per_block, i % per_block
        slot = block % 2

        @pl.when((i < count) & (quarter == 0))
        def _():
            for copy in load(block):
                copy.wait()

            @pl.when(block >= 1)
            def _():
                for copy in store(block - 1):
                    copy.wait()

        half = per_block // 2
        tiles = hidden // TILE // half

        @pl.when((i < count) & (quarter < half))
        def _():
            def tile(t, carry):
                at = pl.ds(pl.multiple_of((quarter * tiles + t) * TILE, TILE), TILE)
                gate = dot_nn(xs[slot], wg[:, at])
                up = dot_nn(xs[slot], wu[:, at])
                back = dot_nn(ogs[slot], wd[:, at])
                sig = jax.nn.sigmoid(gate)
                act = gate * sig
                hs[:, at] = (act * up).astype(BF)
                gs[:, at] = (back * up * sig * (1.0 + gate * (1.0 - sig))).astype(BF)
                us[:, at] = (back * act).astype(BF)
                return carry

            lax.fori_loop(0, tiles, tile, 0)

        @pl.when((i < count) & (quarter >= half))
        def _():
            where = rows_of(block, BLOCK_ROWS)
            tiles_out = acc.shape[1] // TILE // half

            def tile(t, carry):
                at = pl.ds(pl.multiple_of(((quarter - half) * tiles_out + t) * TILE, TILE), TILE)
                acc[where, at] = (dot_nt(gs[...], wg[at, :]) + dot_nt(us[...], wu[at, :])).astype(BF)
                return carry

            lax.fori_loop(0, tiles_out, tile, 0)

        @pl.when((i < count) & (quarter == per_block - 1))
        def _():
            for copy in store(block):
                copy.start()

            @pl.when(block + 2 < blocks)
            def _():
                for copy in load(block + 2):
                    copy.start()

            tree.send_block(block)

        tree.middle_step(i, per_block + 1, per_block + 3, epilogue)
        return carry

    lax.fori_loop(0, count + per_block + 3, step, 0)
    for copy in store(blocks - 1):
        copy.wait()
    tree.drain()

    @pl.when(tree.is_mid)
    def _():
        drop.finish()


def feed_forward(normed_two, out_grad, merged, middle):
    rows, model = normed_two.shape
    hidden = merged.shape[1] // 3
    count = rows // CHUNK
    block = lambda *lead: pltpu.VMEM((*lead, BLOCK_ROWS, model), BF)
    tall = lambda: pltpu.VMEM((model, hidden), BF)
    wide = lambda kind: [pltpu.VMEM((2, CHUNK, model), kind), pltpu.SemaphoreType.DMA((2,))]
    return pl.pallas_call(
        functools.partial(feed_kernel, count),
        out_shape=(
            jax.ShapeDtypeStruct((rows, model), BF),
            jax.ShapeDtypeStruct((rows, model), F32),
            jax.ShapeDtypeStruct((rows, hidden), BF),
            jax.ShapeDtypeStruct((rows, 2 * hidden), BF),
        ),
        in_specs=[ANY] * 4,
        out_specs=(ANY,) * 4,
        scratch_shapes=tree_scratch(rows, model)
        + [tall(), tall(), tall(), pltpu.SemaphoreType.DMA((3,))]
        + [block(2), block(2), pltpu.SemaphoreType.DMA((2, 2))]
        + [pltpu.VMEM((BLOCK_ROWS, hidden), BF) for _ in range(3)]
        + [pltpu.SemaphoreType.DMA((3,))]
        + wide(F32) + wide(BF) + wide(F32),
        compiler_params=params(2),
    )(normed_two, out_grad, merged, middle)


def back_kernel(
    count, groups, heads,
    hid_ref, wf_ref, mid_ref, gb_ref, wo_ref, q_ref, kv_ref, kvo_ref, lse_ref,
    qid_ref, kid_ref, koid_ref, cos_ref, sin_ref,
    out_ref, dqkv_ref,
    acc, from_end, from_mid, *rest,
):
    sems, rest = rest[:6], rest[6:]
    wd, wd_sem, hs, hs_sem, gbs, gbs_sem, mid_slots, mid_sem, ga, probs, gprobs, dkv, dkv_out, dkv_in, dkv_sent, dkv_got = rest
    tree = Tree(count, acc, from_end, from_mid, out_ref, sems)
    mid_feed = Feed(count, mid_ref, mid_slots, mid_sem)
    per_block = BLOCK_ROWS // CHUNK
    blocks = count // per_block
    hidden = wd.shape[1]
    shard_len = q_ref.shape[0] // groups
    width = heads * HD
    root = 1.0 / math.sqrt(HD)
    other = 1 - lax.axis_index("seq")

    def load_hidden(block):
        return pltpu.make_async_copy(
            hid_ref.at[rows_of(block, BLOCK_ROWS)], hs.at[block % 2], hs_sem.at[block % 2]
        )

    def load_branch(block):
        return pltpu.make_async_copy(
            gb_ref.at[rows_of(block, BLOCK_ROWS)], gbs.at[block % 2], gbs_sem.at[block % 2]
        )

    def cross(p):
        return pltpu.make_async_remote_copy(
            dkv_out.at[p], dkv_in.at[p], dkv_sent.at[p], dkv_got.at[p],
            device_id={"seq": other}, device_id_type=MESH,
        )

    weight = pltpu.make_async_copy(wf_ref.at[:, pl.ds(2 * hidden, hidden)], wd, wd_sem.at[0])
    weight.start()
    for block in range(2):
        load_hidden(block).start()
        load_branch(block).start()

    @pl.when(tree.is_mid)
    def _():
        mid_feed.begin()

    tree.barrier(beside_seq=True)
    weight.wait()

    def epilogue(j, total):
        result = (mid_feed.take(j) + total).astype(BF)
        mid_feed.following(j)
        return result

    def pair_back(p):
        group, head = p // heads, p % heads
        where = rows_of(group, shard_len)
        lane = lambda shift: pl.ds(pl.multiple_of((head + shift) * HD, HD), HD)
        queries, grads = q_ref[where, lane(0)], ga[where, lane(0)]
        delta = jnp.zeros((1, shard_len), F32)
        sources = ((kv_ref, kid_ref), (kvo_ref, koid_ref))
        for s, (source, ids) in enumerate(sources):
            at = pl.ds(s * shard_len, shard_len)
            raw = dot_nt(source[where, lane(0)], queries) * root
            prob = jnp.where(ids[group] <= qid_ref[group], jnp.exp(raw - lse_ref[p]), 0.0)
            gprob = dot_nt(source[where, lane(heads)], grads)
            delta = delta + jnp.sum(prob * gprob, axis=0, keepdims=True)
            probs[at] = prob
            gprobs[at] = gprob
        turned = jnp.zeros((HD, shard_len), F32)
        for s, (source, ids) in reversed(list(enumerate(sources))):
            at = pl.ds(s * shard_len, shard_len)
            prob = probs[at]
            graw = (prob * (gprobs[at] - delta) * root).astype(BF)
            gkeys = dot_nn(graw, queries)
            gvalues = dot_nn(prob.astype(BF), grads)
            if s == 1:
                dkv_out[p, :, pl.ds(0, HD)] = gkeys.astype(BF)
                dkv_out[p, :, pl.ds(HD, HD)] = gvalues.astype(BF)
                cross(p).start()
            else:
                dkv[p, :, pl.ds(0, HD)] = gkeys
                dkv[p, :, pl.ds(HD, HD)] = gvalues
            turned = turned + dot_tn(source[where, lane(0)], graw)
        dqkv_ref[where, lane(0)] = turn_back(turned.T).astype(BF)

    def turn_back(values):
        return values * cos_ref[...] + pltpu.roll(values, HD // 2, 1) * sin_ref[...]

    def step(i, carry):
        @pl.when((i % per_block == 0) & (i < count))
        def _():
            block = i // per_block
            where = rows_of(block, BLOCK_ROWS)
            load_hidden(block).wait()
            tiles = acc.shape[1] // (2 * TILE)

            def tile(t, carry):
                at = pl.ds(pl.multiple_of(t * 2 * TILE, 2 * TILE), 2 * TILE)
                acc[where, at] = dot_nt(hs[block % 2], wd[at, :]).astype(BF)
                return carry

            lax.fori_loop(0, tiles, tile, 0)
            tree.send_block(block)

            @pl.when(block + 2 < blocks)
            def _():
                load_hidden(block + 2).start()

        @pl.when(i == 1)
        def _():
            for block in range(blocks):
                load_branch(block).wait()
                ga[rows_of(block, BLOCK_ROWS)] = dot_nn(gbs[block % 2], wo_ref[...]).astype(BF)
                if block + 2 < blocks:
                    load_branch(block + 2).start()

        @pl.when((i >= 2) & (i < 2 + groups * heads))
        def _():
            pair_back(i - 2)

        tree.middle_step(i, 1, 3, epilogue)
        return carry

    lax.fori_loop(0, count + 3, step, 0)

    def gather(p, carry):
        group, head = p // heads, p % heads
        where = rows_of(group, shard_len)
        lane = lambda shift: pl.ds(pl.multiple_of((head + shift) * HD, HD), HD)
        cross(p).wait_recv()
        gkeys = dkv[p, :, pl.ds(0, HD)] + dkv_in[p, :, pl.ds(0, HD)].astype(F32)
        gvalues = dkv[p, :, pl.ds(HD, HD)] + dkv_in[p, :, pl.ds(HD, HD)].astype(F32)
        dqkv_ref[where, lane(heads)] = turn_back(gkeys).astype(BF)
        dqkv_ref[where, lane(2 * heads)] = gvalues.astype(BF)
        cross(p).wait_send()
        return carry

    lax.fori_loop(0, groups * heads, gather, 0)
    tree.drain()


def feed_sum_and_attention_back(
    hidden_low, merged_feed, middle, grad_branch, merged, queries, kv_own, kv_other, lse,
    qid, kid, koid, cosine, sine_back, groups,
):
    rows, hidden = hidden_low.shape
    model, width = middle.shape[1], queries.shape[1]
    heads = width // HD
    count = rows // CHUNK
    shard_len = rows // groups
    pairs = groups * heads
    sem = lambda *shape: pltpu.SemaphoreType.DMA(shape)
    return pl.pallas_call(
        functools.partial(back_kernel, count, groups, heads),
        grid=(1,),
        out_shape=(jax.ShapeDtypeStruct((rows, model), BF), jax.ShapeDtypeStruct((rows, 3 * width), BF)),
        in_specs=[ANY] * 4
        + [pl.BlockSpec((model, width), lambda _: (0, 3))]
        + [VMEM] * 9,
        out_specs=(ANY, VMEM),
        scratch_shapes=tree_scratch(rows, model)
        + [
            pltpu.VMEM((model, hidden), BF), sem(1),
            pltpu.VMEM((2, BLOCK_ROWS, hidden), BF), sem(2),
            pltpu.VMEM((2, BLOCK_ROWS, model), BF), sem(2),
            pltpu.VMEM((2, CHUNK, model), F32), sem(2),
            pltpu.VMEM((rows, width), BF),
            pltpu.VMEM((2 * shard_len, shard_len), F32),
            pltpu.VMEM((2 * shard_len, shard_len), F32),
            pltpu.VMEM((pairs, shard_len, 2 * HD), F32),
            pltpu.VMEM((pairs, shard_len, 2 * HD), BF),
            pltpu.VMEM((pairs, shard_len, 2 * HD), BF),
            sem(pairs), sem(pairs),
        ],
        compiler_params=params(3),
    )(
        hidden_low, merged_feed, middle, grad_branch, merged, queries, kv_own, kv_other, lse,
        qid, kid, koid, cosine, sine_back,
    )


def first_kernel(count, dqkv_ref, w_ref, tok_ref, gm_ref, out_ref, acc, from_end, from_mid, *rest):
    sems, (gm_slots, gm_sem) = rest[:6], rest[6:]
    tree = Tree(count, acc, from_end, from_mid, out_ref, sems)
    feed = Feed(count, gm_ref, gm_slots, gm_sem)
    per_block = BLOCK_ROWS // CHUNK

    @pl.when(tree.is_mid)
    def _():
        feed.begin()

    tree.barrier()

    def epilogue(j, total):
        normed, inverse = norm_parts(tok_ref[rows_of(j, CHUNK)].astype(F32))
        spread = total - jnp.mean(total, axis=-1, keepdims=True)
        grad = inverse * (spread - normed * jnp.mean(total * normed, axis=-1, keepdims=True))
        result = (feed.take(j) + grad).astype(BF)
        feed.following(j)
        return result

    def step(i, carry):
        @pl.when((i % per_block == 0) & (i < count))
        def _():
            block = i // per_block
            where = rows_of(block, BLOCK_ROWS)
            acc[where] = dot_nt(dqkv_ref[where], w_ref[...]).astype(BF)
            tree.send_block(block)

        tree.middle_step(i, 1, 3, epilogue)
        return carry

    lax.fori_loop(0, count + 3, step, 0)
    tree.drain()


def first_sum(dqkv, merged, tokens, grad_middle):
    rows, width = dqkv.shape
    model = tokens.shape[1]
    count = rows // CHUNK
    return pl.pallas_call(
        functools.partial(first_kernel, count),
        grid=(1,),
        out_shape=jax.ShapeDtypeStruct((rows, model), BF),
        in_specs=[VMEM, pl.BlockSpec((model, width), lambda _: (0, 0)), VMEM, ANY],
        out_specs=ANY,
        scratch_shapes=tree_scratch(rows, model)
        + [pltpu.VMEM((2, CHUNK, model), F32), pltpu.SemaphoreType.DMA((2,))],
        compiler_params=params(4),
    )(dqkv, merged, tokens, grad_middle)


def gathered(shard):
    return lax.all_gather(shard, ("dp", "seq"), axis=0, tiled=True)


def scattered(term):
    return lax.psum_scatter(term, ("dp", "seq"), scatter_dimension=0, tiled=True).astype(F32)


def tree_body(
    tokens,
    block_ids,
    query_weight,
    key_weight,
    value_weight,
    out_weight,
    gate_weight,
    up_weight,
    down_weight,
    out_grad,
):
    groups, shard_len, model = tokens.shape
    rows = groups * shard_len
    seq_rank = lax.axis_index("seq")
    merged = gathered(jnp.concatenate([query_weight, key_weight, value_weight, out_weight], axis=1))
    width = query_weight.shape[1]
    heads = width // HD
    feed_shard = jnp.concatenate([gate_weight, up_weight, down_weight], axis=1)
    feed_shard, merged = lax.optimization_barrier((feed_shard, merged))
    merged_feed = gathered(feed_shard)

    positions = (seq_rank * shard_len + jnp.arange(shard_len)).astype(F32)
    cosine, sine = rope_tables(positions)
    sign = jnp.concatenate([jnp.ones((HD // 2,), F32), -jnp.ones((HD // 2,), F32)])
    sine_back = sine * sign
    flat_tokens = tokens.reshape(rows, model)
    normed_low = layer_norm(flat_tokens.astype(F32))[0].astype(BF)

    shape_heads = (groups, shard_len, heads, HD)
    lin_k = matmul(normed_low, merged[:, width : 2 * width]).reshape(shape_heads)
    keys = rotate(lin_k, cosine[None, :, None, :], sine[None, :, None, :]).astype(BF).reshape(rows, width)
    values = matmul(normed_low, merged[:, 2 * width : 3 * width]).astype(BF)
    kv_own = jnp.concatenate([keys, values], axis=1)
    kv_other = lax.ppermute(kv_own, "seq", [(0, 1), (1, 0)])
    lin_q = matmul(normed_low, merged[:, :width]).reshape(shape_heads)
    queries = rotate(lin_q, cosine[None, :, None, :], sine[None, :, None, :]).astype(BF).reshape(rows, width)

    own_ids = lax.dynamic_slice_in_dim(block_ids, seq_rank * shard_len, shard_len, 1)
    other_ids = lax.dynamic_slice_in_dim(block_ids, (1 - seq_rank) * shard_len, shard_len, 1)
    qid, kid, koid = own_ids[:, None, :], own_ids[:, :, None], other_ids[:, :, None]

    attended, lse = attention(queries, kv_own, kv_other, qid, kid, koid, groups, shard_len)
    normed_two, middle = branch_sum(attended, merged, flat_tokens)
    grad_low = out_grad.reshape(rows, model)
    grad_branch, grad_middle, hidden_low, grad_gate_up = feed_forward(
        normed_two, grad_low, merged_feed, middle
    )
    feed_terms = jnp.concatenate(
        [outer_sum(normed_two, grad_gate_up).astype(BF), outer_sum(grad_low, hidden_low).astype(BF)], axis=1
    )
    hidden_low, feed_terms = lax.optimization_barrier((hidden_low, feed_terms))
    feed_grads = scattered(feed_terms)
    output, dqkv = feed_sum_and_attention_back(
        hidden_low, merged_feed, middle, grad_branch, merged, queries, kv_own, kv_other, lse,
        qid, kid, koid, cosine, sine_back, groups,
    )
    head_terms = jnp.concatenate(
        [outer_sum(normed_low, dqkv).astype(BF), outer_sum(grad_branch, attended).astype(BF)], axis=1
    )
    dqkv, head_terms = lax.optimization_barrier((dqkv, head_terms))
    head_grads = scattered(head_terms)
    tokens_grad = first_sum(dqkv, merged, flat_tokens, grad_middle)
    hidden = gate_weight.shape[1]
    return (
        output.reshape(tokens.shape),
        tokens_grad.reshape(tokens.shape),
        head_grads[:, :width],
        head_grads[:, width : 2 * width],
        head_grads[:, 2 * width : 3 * width],
        head_grads[:, 3 * width :],
        feed_grads[:, :hidden],
        feed_grads[:, hidden : 2 * hidden],
        feed_grads[:, 2 * hidden :],
    )


def solution(mesh):
    in_specs = (
        P("dp", "seq", None),
        P("dp", None),
        P(("dp", "seq"), "mp"),
        P(("dp", "seq"), "mp"),
        P(("dp", "seq"), "mp"),
        P(("dp", "seq"), "mp"),
        P(("dp", "seq"), "mp"),
        P(("dp", "seq"), "mp"),
        P(("dp", "seq"), "mp"),
        P("dp", "seq", None),
    )
    out_specs = (
        P("dp", "seq", None),
        P("dp", "seq", None),
        P(("dp", "seq"), "mp"),
        P(("dp", "seq"), "mp"),
        P(("dp", "seq"), "mp"),
        P(("dp", "seq"), "mp"),
        P(("dp", "seq"), "mp"),
        P(("dp", "seq"), "mp"),
        P(("dp", "seq"), "mp"),
    )
    fits = mesh.shape["seq"] == 2 and mesh.shape["mp"] == 4
    body = tree_body if fits else general_body
    return jax.shard_map(body, mesh=mesh, in_specs=in_specs, out_specs=out_specs, check_vma=False)
```

```python
import functools
import math

import jax
import jax.numpy as jnp
import numpy as np
from jax import lax
from jax.experimental import pallas as pl
from jax.experimental.pallas import tpu as pltpu
from jax.sharding import PartitionSpec as P

HD = 128


EPSILON = 1e-05
THETA = 10000.0
MASKED = -1e30


def layer_norm(values):
    centered = values - jnp.mean(values, axis=-1, keepdims=True)
    inverse = lax.rsqrt(jnp.mean(centered * centered, axis=-1, keepdims=True) + EPSILON)
    return (centered * inverse, inverse)


def norm_back(normed, inverse, upstream):
    middle_term = upstream - jnp.mean(upstream, axis=-1, keepdims=True)
    return inverse * (middle_term - normed * jnp.mean(upstream * normed, axis=-1, keepdims=True))


def rope_tables(positions):
    steps_index = jnp.arange(HD // 2).astype(jnp.float32)
    frequency = jnp.exp(steps_index * (-2.0 * math.log(THETA) / HD))
    angles = positions[:, None] * frequency[None, :]
    cosine = jnp.concatenate([jnp.cos(angles), jnp.cos(angles)], axis=-1)
    sine_table = jnp.concatenate([jnp.sin(angles), jnp.sin(angles)], axis=-1)
    return (cosine, sine_table)


def rotate(values, cosine, sine_table):
    halfway = values.shape[-1] // 2
    turned = jnp.concatenate([-values[..., halfway:], values[..., :halfway]], axis=-1)
    return values * cosine + turned * sine_table


def unrotate(values, cosine, sine_table):
    halfway = values.shape[-1] // 2
    scaled = values * sine_table
    turned = jnp.concatenate([scaled[..., halfway:], -scaled[..., :halfway]], axis=-1)
    return values * cosine + turned


def matmul(factor_left, factor_right):
    return jnp.dot(factor_left, factor_right, preferred_element_type=jnp.float32)


def matmul_trans(factor_left, factor_right):
    return lax.dot_general(
        factor_left, factor_right, (((1,), (1,)), ((), ())), preferred_element_type=jnp.float32
    )


def outer_sum(factor_left, factor_right):
    return lax.dot_general(
        factor_left, factor_right, (((0,), (0,)), ((), ())), preferred_element_type=jnp.float32
    )


def general_body(
    tokens,
    block_ids,
    query_weight,
    key_weight,
    value_weight,
    out_weight,
    gate_weight,
    up_weight,
    down_weight,
    out_grad,
):
    groups, shard_len, model_width = tokens.shape
    seq_rank = lax.axis_index("seq")
    seq_len = shard_len * lax.axis_size("seq")
    row_count = groups * shard_len
    shards = (
        query_weight,
        key_weight,
        value_weight,
        out_weight,
        gate_weight,
        up_weight,
        down_weight,
    )
    full_query, full_key, full_value, full_out, full_gate, full_up, full_down = (
        lax.all_gather(shards[0], ("dp", "seq"), axis=0, tiled=True),
        lax.all_gather(shards[1], ("dp", "seq"), axis=0, tiled=True),
        lax.all_gather(shards[2], ("dp", "seq"), axis=0, tiled=True),
        lax.all_gather(shards[3], ("dp", "seq"), axis=0, tiled=True),
        lax.all_gather(shards[4], ("dp", "seq"), axis=0, tiled=True),
        lax.all_gather(shards[5], ("dp", "seq"), axis=0, tiled=True),
        lax.all_gather(shards[6], ("dp", "seq"), axis=0, tiled=True),
    )
    heads_here = full_query.shape[1] // HD
    shape_heads = (groups, shard_len, heads_here, HD)
    score_root = math.sqrt(HD)
    positions = (seq_rank * shard_len + jnp.arange(shard_len)).astype(jnp.float32)
    cosine, sine_table = rope_tables(positions)
    cosine = cosine[None, :, None, :]
    sine_table = sine_table[None, :, None, :]
    inputs = tokens.astype(jnp.float32).reshape(row_count, model_width)
    normed, inverse = layer_norm(inputs)
    normed_low = normed.astype(jnp.bfloat16)
    queries = rotate(
        matmul(normed_low, full_query).reshape(shape_heads), cosine, sine_table
    ).astype(jnp.bfloat16)
    key_local = (
        rotate(matmul(normed_low, full_key).reshape(shape_heads), cosine, sine_table)
        .astype(jnp.bfloat16)
        .reshape(groups, shard_len, -1)
    )
    value_local = matmul(normed_low, full_value).astype(jnp.bfloat16).reshape(groups, shard_len, -1)
    keys_all, values_all = (
        lax.all_gather(key_local, "seq", axis=1, tiled=True),
        lax.all_gather(value_local, "seq", axis=1, tiled=True),
    )
    query_ids = lax.dynamic_slice_in_dim(block_ids, seq_rank * shard_len, shard_len, 1)
    last_ids = query_ids[:, shard_len - 1 :]
    reached = jnp.sum((block_ids <= last_ids).astype(jnp.int32), axis=1)
    key_blocks = (jnp.max(reached) + shard_len - 1) // shard_len

    def block_scores(keys_source, offset):
        key_block = lax.dynamic_slice_in_dim(keys_source, offset, shard_len, 1).reshape(shape_heads)
        raw_scores = jnp.einsum(
            "gqhd,gkhd->ghqk", queries, key_block, preferred_element_type=jnp.float32
        )
        key_ids = lax.dynamic_slice_in_dim(block_ids, offset, shard_len, 1)
        allowed = key_ids[:, None, None, :] <= query_ids[:, None, :, None]
        return (jnp.where(allowed, raw_scores / score_root, MASKED), allowed, key_block)

    def stats_step(block_index, loop_state):
        running_max, running_sum = loop_state
        scores, allowed, key_block = block_scores(keys_all, block_index * shard_len)
        new_max = jnp.maximum(running_max, jnp.max(scores, axis=-1))
        weights_block = jnp.where(allowed, jnp.exp(scores - new_max[..., None]), 0.0)
        return (
            new_max,
            running_sum * jnp.exp(running_max - new_max) + jnp.sum(weights_block, axis=-1),
        )

    stat_shape = (groups, heads_here, shard_len)
    running_max, running_sum = lax.fori_loop(
        0,
        key_blocks,
        stats_step,
        (jnp.full(stat_shape, MASKED, jnp.float32), jnp.zeros(stat_shape, jnp.float32)),
    )
    log_total = running_max + jnp.log(running_sum)

    def output_step(block_index, accumulated):
        offset = block_index * shard_len
        scores, allowed, key_block = block_scores(keys_all, offset)
        weights_block = jnp.where(allowed, jnp.exp(scores - log_total[..., None]), 0.0).astype(
            jnp.bfloat16
        )
        value_block = lax.dynamic_slice_in_dim(values_all, offset, shard_len, 1).reshape(
            shape_heads
        )
        return accumulated + jnp.einsum(
            "ghqk,gkhd->gqhd", weights_block, value_block, preferred_element_type=jnp.float32
        )

    attended = lax.fori_loop(0, key_blocks, output_step, jnp.zeros(shape_heads, jnp.float32))
    attended_low = attended.astype(jnp.bfloat16).reshape(row_count, -1)
    branch = lax.psum(matmul_trans(attended_low, full_out).astype(jnp.bfloat16), "mp").astype(
        jnp.float32
    )
    middle = inputs + branch
    normed_two, inverse_two = layer_norm(middle)
    normed_two_low = normed_two.astype(jnp.bfloat16)
    gate_values = matmul(normed_two_low, full_gate)
    up_values = matmul(normed_two_low, full_up)
    sigmoid_gate = jax.nn.sigmoid(gate_values)
    activated = gate_values * sigmoid_gate
    hidden_low = (activated * up_values).astype(jnp.bfloat16)
    feed_out = lax.psum(matmul_trans(hidden_low, full_down).astype(jnp.bfloat16), "mp").astype(
        jnp.float32
    )
    output = (middle + feed_out).astype(jnp.bfloat16).reshape(groups, shard_len, model_width)
    full_query, full_key, full_value, full_out, full_gate, full_up, full_down = (
        lax.all_gather(shards[0], ("dp", "seq"), axis=0, tiled=True),
        lax.all_gather(shards[1], ("dp", "seq"), axis=0, tiled=True),
        lax.all_gather(shards[2], ("dp", "seq"), axis=0, tiled=True),
        lax.all_gather(shards[3], ("dp", "seq"), axis=0, tiled=True),
        lax.all_gather(shards[4], ("dp", "seq"), axis=0, tiled=True),
        lax.all_gather(shards[5], ("dp", "seq"), axis=0, tiled=True),
        lax.all_gather(shards[6], ("dp", "seq"), axis=0, tiled=True),
    )
    grad_low = out_grad.reshape(row_count, model_width)
    down_term = outer_sum(grad_low, hidden_low)
    grad_hidden = matmul(grad_low, full_down)
    grad_gate = (
        grad_hidden * up_values * sigmoid_gate * (1.0 + gate_values * (1.0 - sigmoid_gate))
    ).astype(jnp.bfloat16)
    grad_up = (grad_hidden * activated).astype(jnp.bfloat16)
    gate_term = outer_sum(normed_two_low, grad_gate)
    up_term = outer_sum(normed_two_low, grad_up)
    grad_normed_two = lax.psum(
        (matmul_trans(grad_gate, full_gate) + matmul_trans(grad_up, full_up)).astype(jnp.bfloat16),
        "mp",
    ).astype(jnp.float32)
    grad_middle = grad_low.astype(jnp.float32) + norm_back(normed_two, inverse_two, grad_normed_two)
    grad_branch = grad_middle.astype(jnp.bfloat16)
    out_term = outer_sum(grad_branch, attended_low)
    grad_attended = matmul(grad_branch, full_out).astype(jnp.bfloat16).reshape(shape_heads)
    row_delta = jnp.einsum("gqhd,gqhd->ghq", grad_attended.astype(jnp.float32), attended)

    def backward_step(block_index, loop_state):
        grad_queries, grad_keys, grad_values = loop_state
        offset = block_index * shard_len
        scores, allowed, key_block = block_scores(keys_all, offset)
        weights_block = jnp.where(allowed, jnp.exp(scores - log_total[..., None]), 0.0)
        value_block = lax.dynamic_slice_in_dim(values_all, offset, shard_len, 1).reshape(
            shape_heads
        )
        grad_weights = jnp.einsum(
            "gqhd,gkhd->ghqk", grad_attended, value_block, preferred_element_type=jnp.float32
        )
        grad_raw = (weights_block * (grad_weights - row_delta[..., None]) / score_root).astype(
            jnp.bfloat16
        )
        grad_queries = grad_queries + jnp.einsum(
            "ghqk,gkhd->gqhd", grad_raw, key_block, preferred_element_type=jnp.float32
        )
        key_part = jnp.einsum(
            "ghqk,gqhd->gkhd", grad_raw, queries, preferred_element_type=jnp.float32
        ).reshape(groups, shard_len, -1)
        value_part = jnp.einsum(
            "ghqk,gqhd->gkhd",
            weights_block.astype(jnp.bfloat16),
            grad_attended,
            preferred_element_type=jnp.float32,
        ).reshape(groups, shard_len, -1)
        grad_keys = lax.dynamic_update_slice_in_dim(grad_keys, key_part, offset, 1)
        grad_values = lax.dynamic_update_slice_in_dim(grad_values, value_part, offset, 1)
        return (grad_queries, grad_keys, grad_values)

    zero_full = jnp.zeros((groups, seq_len, heads_here * HD), jnp.float32)
    grad_queries, grad_keys, grad_values = lax.fori_loop(
        0, key_blocks, backward_step, (jnp.zeros(shape_heads, jnp.float32), zero_full, zero_full)
    )
    grad_key_sum, grad_value_sum = (
        lax.psum_scatter(
            grad_keys.astype(jnp.bfloat16), "seq", scatter_dimension=1, tiled=True
        ).astype(jnp.float32),
        lax.psum_scatter(
            grad_values.astype(jnp.bfloat16), "seq", scatter_dimension=1, tiled=True
        ).astype(jnp.float32),
    )
    grad_q_lin = (
        unrotate(grad_queries, cosine, sine_table).astype(jnp.bfloat16).reshape(row_count, -1)
    )
    grad_k_lin = (
        unrotate(grad_key_sum.reshape(shape_heads), cosine, sine_table)
        .astype(jnp.bfloat16)
        .reshape(row_count, -1)
    )
    grad_v_lin = grad_value_sum.astype(jnp.bfloat16).reshape(row_count, -1)
    query_term = outer_sum(normed_low, grad_q_lin)
    key_term = outer_sum(normed_low, grad_k_lin)
    value_term = outer_sum(normed_low, grad_v_lin)
    grad_partial = (
        matmul_trans(grad_q_lin, full_query)
        + matmul_trans(grad_k_lin, full_key)
        + matmul_trans(grad_v_lin, full_value)
    )
    grad_normed = lax.psum(grad_partial.astype(jnp.bfloat16), "mp").astype(jnp.float32)
    tokens_grad = (
        (grad_middle + norm_back(normed, inverse, grad_normed))
        .astype(jnp.bfloat16)
        .reshape(groups, shard_len, model_width)
    )
    grad_terms = (query_term, key_term, value_term, out_term, gate_term, up_term, down_term)
    query_grad, key_grad, value_grad, out_weight_grad, gate_grad, up_grad, down_grad = (
        lax.psum_scatter(
            grad_terms[0].astype(jnp.bfloat16), ("dp", "seq"), scatter_dimension=0, tiled=True
        ).astype(jnp.float32),
        lax.psum_scatter(
            grad_terms[1].astype(jnp.bfloat16), ("dp", "seq"), scatter_dimension=0, tiled=True
        ).astype(jnp.float32),
        lax.psum_scatter(
            grad_terms[2].astype(jnp.bfloat16), ("dp", "seq"), scatter_dimension=0, tiled=True
        ).astype(jnp.float32),
        lax.psum_scatter(
            grad_terms[3].astype(jnp.bfloat16), ("dp", "seq"), scatter_dimension=0, tiled=True
        ).astype(jnp.float32),
        lax.psum_scatter(
            grad_terms[4].astype(jnp.bfloat16), ("dp", "seq"), scatter_dimension=0, tiled=True
        ).astype(jnp.float32),
        lax.psum_scatter(
            grad_terms[5].astype(jnp.bfloat16), ("dp", "seq"), scatter_dimension=0, tiled=True
        ).astype(jnp.float32),
        lax.psum_scatter(
            grad_terms[6].astype(jnp.bfloat16), ("dp", "seq"), scatter_dimension=0, tiled=True
        ).astype(jnp.float32),
    )
    return (
        output,
        tokens_grad,
        query_grad,
        key_grad,
        value_grad,
        out_weight_grad,
        gate_grad,
        up_grad,
        down_grad,
    )


MESH = pl.DeviceIdType.MESH
ANY = pl.BlockSpec(memory_space=pl.ANY)
VMEM = pl.BlockSpec(memory_space=pltpu.VMEM)
BF = jnp.bfloat16
F32 = jnp.float32
VMEM_LIMIT = 62 * 1024 * 1024
CHUNK = 32
BLOCK_ROWS = 256


def params(collective_id=None):
    if collective_id is None:
        return pltpu.CompilerParams(vmem_limit_bytes=VMEM_LIMIT)
    return pltpu.CompilerParams(
        collective_id=collective_id, has_side_effects=True, vmem_limit_bytes=VMEM_LIMIT
    )


def dot_nt(left, right):
    return lax.dot_general(left, right, (((1,), (1,)), ((), ())), preferred_element_type=F32)


def dot_tn(left, right):
    return lax.dot_general(left, right, (((0,), (0,)), ((), ())), preferred_element_type=F32)


def dot_nn(left, right):
    return jnp.dot(left, right, preferred_element_type=F32)


def rows_of(index, size):
    return pl.ds(pl.multiple_of(index * size, size), size)


def norm_parts(values):
    centered = values - jnp.mean(values, axis=-1, keepdims=True)
    inverse = lax.rsqrt(jnp.mean(centered * centered, axis=-1, keepdims=True) + EPSILON)
    return centered * inverse, inverse


class Tree:
    def __init__(self, chunk, count, acc, from_end, from_mid, out, sems):
        self.chunk = chunk
        self.count, self.acc, self.from_end, self.from_mid, self.out = count, acc, from_end, from_mid, out
        self.slots = acc.shape[0] // chunk
        self.sent, self.got_end, self.got_mid, self.fin_sent, self.fin_got, self.fin_kept = sems
        position = lax.axis_index("mp")
        self.outer = position + 1 - 2 * (position % 2)
        self.peer = 3 - position
        self.is_mid = (position + 1) // 2 == 1
        self.is_end = (position + 1) // 2 != 1

    def barrier(self, beside_seq=False, extra=0):
        barrier = pltpu.get_barrier_semaphore()
        pl.semaphore_signal(barrier, inc=1, device_id={"mp": self.outer}, device_id_type=MESH)

        @pl.when(self.is_mid)
        def _():
            pl.semaphore_signal(barrier, inc=1, device_id={"mp": self.peer}, device_id_type=MESH)

        position = lax.axis_index("mp")
        pl.semaphore_wait(barrier, 1 + extra + (position * (3 - position)) // 2)

    def slot(self, j):
        return rows_of(j % self.slots, self.chunk)

    def part(self, j):
        return pltpu.make_async_remote_copy(
            self.acc.at[self.slot(j)], self.from_end.at[self.slot(j)], self.sent.at[j % self.slots], self.got_end.at[j % self.slots],
            device_id={"mp": self.outer}, device_id_type=MESH,
        )

    def pair(self, j):
        return pltpu.make_async_remote_copy(
            self.acc.at[self.slot(j)], self.from_mid.at[self.slot(j)], self.sent.at[j % self.slots], self.got_mid.at[j % self.slots],
            device_id={"mp": self.peer}, device_id_type=MESH,
        )

    def final(self, j):
        return pltpu.make_async_remote_copy(
            self.acc.at[self.slot(j)], self.out.at[rows_of(j, self.chunk)], self.fin_sent.at[j % self.slots], self.fin_got.at[j % self.slots],
            device_id={"mp": self.outer}, device_id_type=MESH,
        )

    def keep(self, j):
        return pltpu.make_async_copy(
            self.acc.at[self.slot(j)], self.out.at[rows_of(j, self.chunk)], self.fin_kept.at[j % self.slots]
        )

    def send_block(self, block):
        per_block = BLOCK_ROWS // self.chunk

        @pl.when(self.is_end)
        def _():
            for s in range(per_block):
                self.part(block * per_block + s).start()

    def settle(self, first, amount):
        @pl.when(self.is_end)
        def _():
            def one(s, carry):
                self.part(first + s).wait_send()
                self.final(first + s).wait_recv()
                return carry

            lax.fori_loop(0, amount, one, 0)

        @pl.when(self.is_mid)
        def _():
            def one(s, carry):
                self.final(first + s).wait_send()
                self.keep(first + s).wait()
                return carry

            lax.fori_loop(0, amount, one, 0)

    def middle_step(self, i, lag_sum, lag_final, epilogue, first=0, last=None):
        last = self.count if last is None else last
        j = i - lag_sum

        @pl.when(self.is_mid & (j >= first) & (j < last))
        def _():
            self.part(j).wait_recv()
            where = self.slot(j)
            self.acc[where] = (self.acc[where].astype(F32) + self.from_end[where].astype(F32)).astype(BF)
            self.pair(j).start()

        k = i - lag_final

        @pl.when(self.is_mid & (k >= first) & (k < last))
        def _():
            self.pair(k).wait_recv()
            where = self.slot(k)
            total = self.acc[where].astype(F32) + self.from_mid[where].astype(F32)
            result = epilogue(k, total)
            self.pair(k).wait_send()
            self.acc[where] = result
            self.final(k).start()
            self.keep(k).start()

    def drain(self):
        self.settle(self.count - self.slots, self.slots)


class Feed:
    def __init__(self, chunk, count, source, slots, sem):
        self.chunk, self.count, self.source, self.slots, self.sem = chunk, count, source, slots, sem

    def copy(self, j):
        return pltpu.make_async_copy(
            self.source.at[rows_of(j, self.chunk)], self.slots.at[j % 2], self.sem.at[j % 2]
        )

    def begin(self):
        self.copy(0).start()
        self.copy(1).start()

    def take(self, j):
        self.copy(j).wait()
        return self.slots[j % 2]

    def following(self, j):
        @pl.when(j + 2 < self.count)
        def _():
            self.copy(j + 2).start()


class Drop:
    def __init__(self, chunk, count, target, slots, sem):
        self.chunk, self.count, self.target, self.slots, self.sem = chunk, count, target, slots, sem

    def copy(self, j):
        return pltpu.make_async_copy(
            self.slots.at[j % 2], self.target.at[rows_of(j, self.chunk)], self.sem.at[j % 2]
        )

    def put(self, j, values):
        @pl.when(j >= 2)
        def _():
            self.copy(j - 2).wait()

        self.slots[j % 2] = values
        self.copy(j).start()

    def finish(self):
        self.copy(self.count - 2).wait()
        self.copy(self.count - 1).wait()


def tree_scratch(chunk, held_rows, width):
    buffers = [pltpu.VMEM((held_rows, width), BF) for _ in range(3)]
    return buffers + [pltpu.SemaphoreType.DMA((held_rows // chunk,)) for _ in range(6)]


class Plane:
    def __init__(self):
        dp, self.y = lax.axis_index("dp"), lax.axis_index("seq")
        self.x, self.core = dp // 2, dp % 2
        self.sibling = {"dp": self.x * 2 + 1 - self.core}
        self.x_next = {"dp": (1 - self.x) * 2 + self.core}
        self.y_next = {"seq": 1 - self.y}

    def greet(self):
        barrier = pltpu.get_barrier_semaphore()
        for device in (self.sibling, self.x_next, self.y_next):
            pl.semaphore_signal(barrier, inc=1, device_id=device, device_id_type=MESH)

    def block_at(self, r, core):
        over_x, over_y = r // 2, r % 2
        x = self.x + over_x * (1 - 2 * self.x)
        y = self.y + over_y * (1 - 2 * self.y)
        return (x * 2 + core) * 2 + y


class Gather:
    def __init__(self, plane, out, own_rows, width, sent, got):
        self.plane, self.out, self.own_rows, self.width, self.sent, self.got = plane, out, own_rows, width, sent, got

    def piece(self, m, kind):
        plane, part = self.plane, self.width // 4
        r, device, shift, size = (
            (0, plane.sibling, 0, self.width),
            (0, plane.x_next, 0, self.width),
            (0, plane.y_next, 0, self.width),
            (1, plane.x_next, 0, self.width if self.early(m) else 3 * part),
            (2, plane.y_next, 3 * part, part),
            (2, plane.sibling, 0, self.width),
            (1, plane.sibling, 0, self.width),
            (3, plane.sibling, 0, self.width),
        )[kind]
        at = pl.ds(pl.multiple_of(m * self.width + shift, part), size)
        window = self.out.at[rows_of(plane.block_at(r, plane.core), BLOCK_ROWS), at]
        return pltpu.make_async_remote_copy(
            self.own_rows.at[:, at] if kind < 3 else window, window, self.sent.at[kind, m], self.got.at[kind, m],
            device_id=device, device_id_type=MESH,
        )

    def early(self, m):
        return isinstance(m, int) and m < 4

    def own_x(self, m):
        self.piece(m, 1).start()
        self.piece(m, 0).start()

    def own_y(self, m):
        self.piece(m, 2).start()

    def relay_x(self, m):
        self.piece(m, 1).wait_recv()
        if not self.early(m):
            self.piece(m, 4).start()
        self.piece(m, 5).start()

    def relay_y(self, m):
        self.piece(m, 2).wait_recv()
        self.piece(m, 3).start()
        self.piece(m, 6).start()

    def corner(self, m):
        self.piece(m, 3).wait_recv()
        if not self.early(m):
            self.piece(m, 4).wait_recv()
        self.piece(m, 7).start()

    def complete(self, m):
        for kind in (0, 5, 6, 7):
            self.piece(m, kind).wait_recv()

    def settle(self, m):
        for kind in range(8):
            if kind != 4 or not self.early(m):
                self.piece(m, kind).wait_send()


class Scatter:
    def __init__(self, plane, count, width, product, out, work, sums, from_x, from_y, buffers):
        (
            self.diag_x, self.diag_y, self.staged,
            self.sib_sent, self.sib_got, self.credit, self.sent, self.got, self.out_sem,
        ) = buffers
        self.plane, self.count, self.width, self.product, self.out = plane, count, width, product, out
        self.work, self.all_sums, self.all_x, self.all_y = work, sums, from_x, from_y
        self.half = width // 2

    def lanes(self, index, shift=0, size=None):
        return pl.ds(pl.multiple_of(index * self.width + shift, self.half), self.width if size is None else size)

    def sums(self, k, r, shift=0, size=None):
        return self.all_sums.at[:, self.lanes((k % 4) * 4 + r, shift, size)]

    def from_x(self, k, shift=0, size=None):
        return self.all_x.at[(k % 8) // 4, :, self.lanes(k % 4, shift, size)]

    def from_y(self, k, shift=0, size=None):
        return self.all_y.at[(k % 8) // 4, :, self.lanes(k % 4, shift, size)]

    def to_sibling(self, k):
        return pltpu.make_async_remote_copy(
            self.work.at[k % 2], self.work.at[2 + k % 2], self.sib_sent.at[k % 2], self.sib_got.at[k % 2],
            device_id=self.plane.sibling, device_id_type=MESH,
        )

    def piece(self, k, kind):
        half, x_next, y_next = self.half, self.plane.x_next, self.plane.y_next
        source, target, device = (
            (self.sums(k, 3, 0, half), self.diag_x.at[k % 8], x_next),
            (self.sums(k, 3, half, half), self.diag_y.at[k % 8], y_next),
            (self.sums(k, 2, 0, half), self.from_x(k, 0, half), x_next),
            (self.sums(k, 1, half, half), self.from_y(k, half, half), y_next),
            (self.sums(k, 1, 0, half), self.from_y(k, 0, half), y_next),
            (self.sums(k, 2, half, half), self.from_x(k, half, half), x_next),
        )[kind]
        return pltpu.make_async_remote_copy(
            source, target, self.sent.at[kind, k % 8], self.got.at[kind, k % 8],
            device_id=device, device_id_type=MESH,
        )

    def keep(self, k):
        return pltpu.make_async_copy(self.staged.at[k % 2], self.out.at[:, self.lanes(k)], self.out_sem.at[k % 2])

    def ready(self):
        for _ in range(2):
            pl.semaphore_signal(self.credit, inc=1, device_id=self.plane.sibling, device_id_type=MESH)

    def compute(self, k):
        @pl.when((k >= 2) & (k < self.count))
        def _():
            self.to_sibling(k - 2).wait_send()

        @pl.when((k >= 0) & (k < self.count))
        def _():
            plane, rows = self.plane, self.staged.shape[1]

            def both(x, core):
                result = self.product(k, 2 * x + core).astype(BF)
                over_x = x + plane.x - 2 * x * plane.x
                return [(2 * over_x + y + plane.y - 2 * y * plane.y, result[y * rows : (y + 1) * rows]) for y in range(2)]

            def theirs(x, carry):
                for r, values in both(x, 1 - plane.core):
                    self.work[k % 2, :, self.lanes(r)] = values
                return carry

            lax.fori_loop(0, 2, theirs, 0)
            pl.semaphore_wait(self.credit, 1)
            self.to_sibling(k).start()

            def ours(x, carry):
                for r, values in both(x, plane.core):
                    self.sums(k, r)[...] = values
                return carry

            lax.fori_loop(0, 2, ours, 0)

    def join_cores(self, k):
        @pl.when((k >= 0) & (k < self.count))
        def _():
            self.to_sibling(k).wait_recv()

            def one(r, carry):
                at = 3 - r
                self.sums(k, at)[...] = (
                    self.sums(k, at)[...].astype(F32) + self.work[2 + k % 2, :, self.lanes(at)].astype(F32)
                ).astype(BF)
                return carry

            lax.fori_loop(0, 4, one, 0)

            @pl.when(k + 2 < self.count)
            def _():
                pl.semaphore_signal(self.credit, inc=1, device_id=self.plane.sibling, device_id_type=MESH)

            for kind in range(4):
                self.piece(k, kind).start()

    def join_diagonal(self, k):
        half = self.half

        @pl.when((k >= 0) & (k < self.count))
        def _():
            self.piece(k, 0).wait_recv()
            target = self.sums(k, 1, 0, half)
            target[...] = (target[...].astype(F32) + self.diag_x[k % 8].astype(F32)).astype(BF)
            self.piece(k, 4).start()
            self.piece(k, 1).wait_recv()
            target = self.sums(k, 2, half, half)
            target[...] = (target[...].astype(F32) + self.diag_y[k % 8].astype(F32)).astype(BF)
            self.piece(k, 5).start()

    def finish(self, k):
        @pl.when((k >= 0) & (k < self.count))
        def _():
            for kind in (2, 3, 4, 5):
                self.piece(k, kind).wait_recv()

            @pl.when(k >= 2)
            def _():
                self.keep(k - 2).wait()

            self.staged[k % 2] = (
                self.sums(k, 0)[...].astype(F32)
                + self.from_x(k)[...].astype(F32)
                + self.from_y(k)[...].astype(F32)
            )
            self.keep(k).start()
            for kind in range(6):
                self.piece(k, kind).wait_send()

    def drain(self):
        for k in (self.count - 2, self.count - 1):
            self.keep(k).wait()
            self.to_sibling(k).wait_send()


def scatter_scratch(rows, width):
    sem = lambda *shape: pltpu.SemaphoreType.DMA(shape)
    return [
        pltpu.VMEM((8, rows, width // 2), BF),
        pltpu.VMEM((8, rows, width // 2), BF),
        pltpu.VMEM((4, rows, width), F32),
        sem(2), sem(2), pltpu.SemaphoreType.REGULAR, sem(6, 8), sem(6, 8), sem(2),
    ]


def layer_kernel(
    chunk, count, groups, heads,
    tok_ref, q_w, k_w, v_w, o_w, g_w, u_w, d_w, og_ref, ids_ref, cos_ref, sin_ref,
    full_ref, n1_ref, rows_ref, mid_ref, gm_ref, hid_ref, ggu_ref, part_ref, grads_ref,
    acc, from_end, from_mid, *rest,
):
    sems, rest = rest[:6], rest[6:]
    (
        mid_slots, mid_sem, tok_slots, tok_sem, res_slots, res_sem, og_slots, og_sem, gm_sem,
        wg, wu, wd, load_sem, xs, ogs, in_sem, work, out_sem,
        n1_sem, w_sem, own, own_sem, q_s, kv_s, kvo_s, att_s, lse_s, kv_sent, kv_got, g_sent, g_got,
        lhs_sem, rhs_sem, dkv_sent, dkv_got, ready_x, ready_y, rows_s, columns_s, cos_s, sin_s, table_sem,
    ) = rest[:42]
    scatter_buffers = rest[42:]
    hs, gs, us, ps = (work.at[s] for s in range(4))
    shards = (q_w, k_w, v_w, o_w, g_w, u_w, d_w)
    wide, hidden = q_w.shape[1], g_w.shape[1]
    per_sum = count // 4
    tree = Tree(chunk, count, acc, from_end, from_mid, rows_ref, sems)
    drop = Drop(chunk, per_sum, mid_ref, mid_slots, mid_sem)
    tok_feed = Feed(chunk, per_sum, tok_ref, tok_slots, tok_sem)
    og_feed = Feed(chunk, per_sum, og_ref, og_slots, og_sem)
    gm_drop = Drop(chunk, per_sum, gm_ref, mid_slots, gm_sem)
    plane = Plane()
    gather = Gather(plane, full_ref, own, wide, g_sent, g_got)
    shard_len = per_sum * chunk // groups
    per_block = BLOCK_ROWS // chunk
    blocks = per_sum // per_block
    group_blocks = blocks // groups
    pairs = groups * heads
    tiles = hidden // wide
    root = 1.0 / math.sqrt(HD)
    rows = per_sum * chunk
    own_rows = rows_of(plane.block_at(0, plane.core), BLOCK_ROWS)
    n1 = wd.at[pl.ds(0, per_sum * chunk)]
    wbuf = [wu.at[:, pl.ds(hidden - 2 * wide, wide)], wu.at[:, pl.ds(hidden - wide, wide)]]

    def load_tokens(block):
        return pltpu.make_async_copy(
            tok_ref.at[rows_of(block, BLOCK_ROWS)], xs.at[block % 2], in_sem.at[0, block % 2]
        )

    def save_normed(block):
        where = rows_of(block, BLOCK_ROWS)
        return pltpu.make_async_copy(n1.at[where], n1_ref.at[where], n1_sem.at[block])

    own_loads, column = [], 0
    for s, shard in enumerate(shards):
        size = shard.shape[1]
        own_loads.append(pltpu.make_async_copy(shard, own.at[:, pl.ds(column, size)], own_sem.at[s]))
        column += size
    own_save = pltpu.make_async_copy(own, full_ref.at[own_rows], own_sem.at[len(shards)])
    feeds = 3 * tiles

    def feed_chunk(n):
        return 4 + (n % 3) * tiles + n // 3

    def load_weight(m, slot):
        return pltpu.make_async_copy(full_ref.at[:, pl.ds(m * wide, wide)], wbuf[slot], w_sem.at[slot])

    def load_feed(n, which):
        m, at = feed_chunk(n), pl.ds(pl.multiple_of((n // 3) * wide, wide), wide)
        return pltpu.make_async_copy(
            full_ref.at[:, pl.ds(pl.multiple_of(m * wide, wide), wide)],
            (wg, wu, wd)[which].at[:, at],
            load_sem.at[n],
        )

    def fill(n):
        gather.complete(feed_chunk(n))
        for which in range(3):
            @pl.when(n % 3 == which)
            def _():
                load_feed(n, which).start()

    def cross(p, part):
        at = pl.ds(part * HD, HD)
        return pltpu.make_async_remote_copy(
            kv_s.at[p, :, at], kvo_s.at[p, :, at], kv_sent.at[part, p], kv_got.at[part, p],
            device_id=plane.y_next, device_id_type=MESH,
        )

    for block in range(2):
        load_tokens(block).start()
    for copy in own_loads:
        copy.start()
    tables = [
        pltpu.make_async_copy(source.at[plane.y], target, table_sem.at[s])
        for s, (source, target) in enumerate(((cos_ref, cos_s), (sin_ref, sin_s)))
    ]
    for copy in tables:
        copy.start()
    plane.greet()
    tree.barrier(extra=3)
    for s in range(4):
        own_loads[s].wait()
    gather.own_x(1)
    gather.own_x(2)
    for m in (1, 2, 0, 3):
        gather.own_y(m)
    for s in range(4, len(shards)):
        own_loads[s].wait()
    own_save.start()

    @pl.when(tree.is_mid)
    def _():
        tok_feed.begin()

    for group in range(groups):
        for s, rank in enumerate((plane.y, 1 - plane.y)):
            ids = ids_ref[group : group + 1, rows_of(rank, shard_len)].astype(F32)
            columns_s[s, group] = jnp.broadcast_to(ids, (HD, shard_len)).T.astype(BF)
            if s == 0:
                rows_s[group] = jnp.broadcast_to(ids, (8, shard_len))

    def allowed(s, group):
        return columns_s[s, group].astype(F32)[:, :1] <= rows_s[group][:1]

    for block in range(blocks):
        load_tokens(block).wait()
        n1[rows_of(block, BLOCK_ROWS)] = norm_parts(xs[block % 2].astype(F32))[0].astype(BF)
        save_normed(block).start()
        if block + 2 < blocks:
            load_tokens(block + 2).start()
        if block == 1:
            gather.relay_y(1)
            gather.relay_x(1)
    own_save.wait()
    for copy in tables:
        copy.wait()

    def turn(values):
        return values * cos_s[...] + pltpu.roll(values, HD // 2, 1) * sin_s[...]

    def fetch(m, slot):
        gather.complete(m)
        load_weight(m, slot).start()

    def project(slot, group, put):
        lin = dot_nn(n1[rows_of(group, shard_len)], wbuf[slot][...])
        for head in range(heads):
            put(group * heads + head, lin[:, head * HD : (head + 1) * HD])

    def put_key(p, values):
        kv_s[p, :, pl.ds(0, HD)] = turn(values).astype(BF)
        cross(p, 0).start()

    def put_value(p, values):
        kv_s[p, :, pl.ds(HD, HD)] = values.astype(BF)
        cross(p, 1).start()

    def put_query(p, values):
        q_s[p] = turn(values).astype(BF)

    gather.relay_y(2)
    gather.relay_x(2)
    gather.own_x(0)
    gather.corner(1)
    gather.relay_y(0)
    fetch(1, 0)
    load_weight(1, 0).wait()
    project(0, 0, put_key)
    gather.own_x(3)
    gather.corner(2)
    gather.relay_y(3)
    gather.own_x(feed_chunk(0))
    gather.own_x(feed_chunk(1))
    fetch(2, 1)
    load_weight(2, 1).wait()
    project(1, 0, put_value)
    for group in range(1, groups):
        project(0, group, put_key)
        project(1, group, put_value)
    gather.own_y(feed_chunk(0))
    gather.relay_x(0)
    gather.corner(0)
    gather.own_x(feed_chunk(2))
    fetch(0, 0)
    load_weight(0, 0).wait()
    for group in range(groups):
        project(0, group, put_query)
    gather.relay_x(3)
    gather.corner(3)
    gather.own_x(feed_chunk(3))
    gather.own_y(feed_chunk(1))
    fetch(3, 1)
    gather.own_x(feed_chunk(4))
    gather.own_y(feed_chunk(2))
    for block in range(blocks):
        save_normed(block).wait()

    def attend(p):
        group, head = p // heads, p % heads
        queries = q_s[p]

        def scores(keys, s):
            return jnp.where(allowed(s, group), dot_nt(keys, queries) * root, MASKED)

        own_part = scores(kv_s[p, :, pl.ds(0, HD)], 0)
        cross(p, 0).wait_recv()
        other = scores(kvo_s[p, :, pl.ds(0, HD)], 1)
        top = jnp.maximum(jnp.max(own_part, axis=0, keepdims=True), jnp.max(other, axis=0, keepdims=True))
        own_part, other = jnp.exp(own_part - top), jnp.exp(other - top)
        total = jnp.sum(own_part, axis=0, keepdims=True) + jnp.sum(other, axis=0, keepdims=True)
        scale = 1.0 / total
        mixed = dot_tn(kv_s[p, :, pl.ds(HD, HD)], (own_part * scale).astype(BF))
        cross(p, 1).wait_recv()
        mixed = mixed + dot_tn(kvo_s[p, :, pl.ds(HD, HD)], (other * scale).astype(BF))
        lane = pl.ds(pl.multiple_of(head * HD, HD), HD)
        att_s[rows_of(group, shard_len), lane] = mixed.T.astype(BF)
        lse_s[p] = top + jnp.log(total)

    held = tree.slots // per_block

    def project_out(block):
        acc[rows_of(block % held, BLOCK_ROWS)] = dot_nt(
            att_s[rows_of(block, BLOCK_ROWS)], wbuf[1][...]
        ).astype(BF)
        tree.send_block(block)

    def first_pairs(p, carry):
        attend(p)
        return carry

    lax.fori_loop(0, heads, first_pairs, 0)
    load_weight(3, 1).wait()
    for block in range(held):
        project_out(block)

    def first_epilogue(j, total):
        middle = tok_feed.take(j).astype(F32) + total
        tok_feed.following(j)
        drop.put(j, middle)
        return norm_parts(middle)[0].astype(BF)

    def second_epilogue(j, total):
        row = j - per_sum
        residual(j).wait()
        normed, inverse = norm_parts(res_slots[j % 2])
        grad_low = og_feed.take(row).astype(F32)
        spread = total - jnp.mean(total, axis=-1, keepdims=True)
        grad = grad_low + inverse * (spread - normed * jnp.mean(total * normed, axis=-1, keepdims=True))
        residual_start(j + 2)
        og_feed.following(row)
        gm_drop.put(row, grad)
        return grad.astype(BF)

    def residual(j):
        return pltpu.make_async_copy(
            mid_ref.at[rows_of(j % per_sum, chunk)], res_slots.at[j % 2], res_sem.at[j % 2]
        )

    def residual_start(j):
        @pl.when(j < 3 * per_sum)
        def _():
            residual(j).start()

        @pl.when((j >= 3 * per_sum) & (j < count))
        def _():
            pltpu.make_async_copy(
                gm_ref.at[rows_of(j % per_sum, chunk)], res_slots.at[j % 2], res_sem.at[j % 2]
            ).start()

    def third_epilogue(j, total):
        residual(j).wait()
        result = (res_slots[j % 2] + total).astype(BF)
        residual_start(j + 2)
        return result

    def fourth_epilogue(j, total):
        row = j - 3 * per_sum
        normed, inverse = norm_parts(tok_feed.take(row).astype(F32))
        tok_feed.following(row)
        spread = total - jnp.mean(total, axis=-1, keepdims=True)
        grad = inverse * (spread - normed * jnp.mean(total * normed, axis=-1, keepdims=True))
        residual(j).wait()
        result = (res_slots[j % 2] + grad).astype(BF)
        residual_start(j + 2)
        return result

    def load_block(block):
        where, slot = rows_of(block, BLOCK_ROWS), block % 2
        return (
            pltpu.make_async_copy(rows_ref.at[where], xs.at[slot], in_sem.at[0, slot]),
            pltpu.make_async_copy(og_ref.at[where], ogs.at[slot], in_sem.at[1, slot]),
        )

    def store_block(block):
        where = rows_of(block, BLOCK_ROWS)
        return (
            pltpu.make_async_copy(hs, hid_ref.at[where], out_sem.at[0]),
            pltpu.make_async_copy(gs, ggu_ref.at[where, pl.ds(0, hidden)], out_sem.at[1]),
            pltpu.make_async_copy(us, ggu_ref.at[where, pl.ds(hidden, hidden)], out_sem.at[2]),
            pltpu.make_async_copy(ps, part_ref.at[where], out_sem.at[3]),
        )

    per_feed = hidden // wide
    starts = (0, 2 * per_feed, 3 * per_feed, 3 * per_feed + 1)
    lefts = (rows_ref.at[pl.ds(0, rows)], og_ref, rows_ref.at[pl.ds(rows, rows)], n1_ref)
    dqkv, ga = wd.at[pl.ds(0, rows), pl.ds(0, 3 * wide)], wd.at[pl.ds(0, rows), pl.ds(3 * wide, wide)]
    rights = (ggu_ref, hid_ref, att_s, dqkv)
    weights = wu.at[:, pl.ds(0, 3 * wide)]

    def left_copy(p):
        return pltpu.make_async_copy(lefts[p], wg.at[pl.ds((p % 2) * rows, rows)], lhs_sem.at[p % 2])

    out_weight = pltpu.make_async_copy(
        full_ref.at[:, pl.ds(3 * wide, wide)], wu.at[:, pl.ds(0, wide)], w_sem.at[0]
    )
    head_weights = pltpu.make_async_copy(full_ref.at[:, pl.ds(0, 3 * wide)], weights, w_sem.at[1])

    def phase(k):
        return sum((k >= start).astype(jnp.int32) for start in starts[1:])

    def right_slot(k):
        return (rows_of(k % 2, rows), pl.ds(3 * wide, wide))

    def right_copy(k, p):
        at = pl.ds(pl.multiple_of((k - starts[p]) * wide, wide), wide)
        return pltpu.make_async_copy(rights[p].at[:, at], wu.at[right_slot(k)], rhs_sem.at[k % 2])

    def right_arrived(k):
        pltpu.make_async_copy(att_s, wu.at[right_slot(k)], rhs_sem.at[k % 2]).wait()

    def right_start(k):
        for p in range(4):
            last = starts[p + 1] if p < 3 else columns

            @pl.when((k >= starts[p]) & (k < last))
            def _():
                right_copy(k, p).start()

    def product(k, block_pair):
        at = rows_of(block_pair, 2 * BLOCK_ROWS)
        return dot_tn(wg[rows_of(phase(k) % 2, rows), at], wu[right_slot(k)])

    columns = starts[3] + 3
    scatter = Scatter(plane, columns, wide, product, grads_ref, work, own, xs, ogs, scatter_buffers)

    def load_part(block):
        return pltpu.make_async_copy(
            part_ref.at[rows_of(block, BLOCK_ROWS)], acc.at[rows_of(block % held, BLOCK_ROWS)], load_sem.at[0]
        )

    def far_grads(p, shift):
        return wd.at[
            pl.ds(pl.multiple_of(rows + (p // heads) * shard_len, shard_len), shard_len),
            pl.ds(pl.multiple_of((p % heads) * 2 * HD + shift, 2 * HD), 2 * HD),
        ]

    def cross_back(p):
        return pltpu.make_async_remote_copy(
            far_grads(p, heads * 2 * HD), far_grads(p, 0), dkv_sent.at[p], dkv_got.at[p],
            device_id=plane.y_next, device_id_type=MESH,
        )

    def turn_back(values):
        return values * cos_s[...] - pltpu.roll(values, HD // 2, 1) * sin_s[...]

    def lane(index):
        return pl.ds(pl.multiple_of(index * HD, HD), HD)

    def group_grads(group):
        for b in range(group_blocks):
            at = rows_of(group * group_blocks + b, BLOCK_ROWS)
            ga[at] = dot_nn(wg[pl.ds(rows + (group * group_blocks + b) * BLOCK_ROWS, BLOCK_ROWS)], wu[:, pl.ds(0, wide)]).astype(BF)

    def pair_back(p):
        group, head = p // heads, p % heads
        where = rows_of(group, shard_len)
        queries, grads = q_s[p], ga[where, lane(head)]
        weighed = grads.astype(F32) * att_s[where, lane(head)].astype(F32)
        delta = jnp.sum(weighed.T, axis=0, keepdims=True)
        turned = jnp.zeros((HD, shard_len), F32)
        for mine, source in ((False, kvo_s), (True, kv_s)):
            raw = dot_nt(source[p, :, pl.ds(0, HD)], queries) * root
            prob = jnp.where(allowed(0 if mine else 1, group), jnp.exp(raw - lse_s[p]), 0.0)
            gprob = dot_nt(source[p, :, pl.ds(HD, HD)], grads)
            graw = (prob * (gprob - delta) * root).astype(BF)
            gkeys = dot_nn(graw, queries).astype(BF)
            gvalues = dot_nn(prob.astype(BF), grads).astype(BF)
            if mine:
                dqkv[where, lane(heads + head)] = gkeys
                dqkv[where, lane(2 * heads + head)] = gvalues
            else:
                target = far_grads(p, heads * 2 * HD)
                target[:, pl.ds(0, HD)] = gkeys
                target[:, pl.ds(HD, HD)] = gvalues
                cross_back(p).start()
            turned = turned + dot_tn(source[p, :, pl.ds(0, HD)], graw)
        dqkv[where, lane(head)] = turn_back(turned.T).astype(BF)

    def pair_join(p):
        group, head = p // heads, p % heads
        where = rows_of(group, shard_len)
        cross_back(p).wait_recv()
        source = far_grads(p, 0)
        gkeys = dqkv[where, lane(heads + head)].astype(F32) + source[:, pl.ds(0, HD)].astype(F32)
        gvalues = dqkv[where, lane(2 * heads + head)].astype(F32) + source[:, pl.ds(HD, HD)].astype(F32)
        dqkv[where, lane(heads + head)] = turn_back(gkeys).astype(BF)
        dqkv[where, lane(2 * heads + head)] = gvalues.astype(BF)
        cross_back(p).wait_send()

    def leave(m, carry):
        gather.settle(m)
        return carry

    early_sum = scatter_buffers[2]
    lag = per_block + 1
    attend_at = lag
    third_at, fourth_at = attend_at + heads, 2 * per_block + 3
    feed_at = per_sum
    turn_at = 2 * per_sum

    def step(i, carry):
        tree.middle_step(i, 1, 3, first_epilogue, 0, per_sum)
        tree.middle_step(i, lag, lag + 2, second_epilogue, per_sum, 2 * per_sum)
        tree.middle_step(i, lag, lag + 2, third_epilogue, 2 * per_sum, 3 * per_sum)
        tree.middle_step(i, lag, lag + 2, fourth_epilogue, 3 * per_sum, count)

        @pl.when((i >= 7) & (i % 2 == 1))
        def _():
            n = (i - 7) // 2

            @pl.when(n + 5 < feeds)
            def _():
                gather.own_x(feed_chunk(n + 5))

            @pl.when(n + 3 < feeds)
            def _():
                gather.own_y(feed_chunk(n + 3))

            @pl.when(n < feeds)
            def _():
                gather.relay_x(feed_chunk(n))
                gather.relay_y(feed_chunk(n))

            @pl.when((n >= 2) & (n - 2 < feeds))
            def _():
                gather.corner(feed_chunk(n - 2))

            @pl.when((n >= 4) & (n - 4 < feeds - 3))
            def _():
                fill(n - 4)

        @pl.when((i >= attend_at) & (i < attend_at + heads))
        def _():
            attend(heads + i - attend_at)

        @pl.when(i == third_at)
        def _():
            tree.settle(0, per_block)
            project_out(held)

        @pl.when(i == fourth_at)
        def _():
            tree.settle(per_block, per_block)
            project_out(held + 1)
            for block in range(2):
                for copy in load_block(block):
                    copy.start()

        at_feed = i - feed_at
        block, part = at_feed // per_block, at_feed % per_block
        slot = block % 2
        half = per_block // 2
        running = (at_feed >= 0) & (at_feed < per_sum)

        @pl.when(i == feed_at + half)
        def _():
            @pl.when(tree.is_mid)
            def _():
                drop.finish()
                residual_start(per_sum)
                residual_start(per_sum + 1)
                og_feed.begin()

        @pl.when(running & (part == 0))
        def _():
            for copy in load_block(block):
                copy.wait()

            @pl.when(block >= 1)
            def _():
                for copy in store_block(block - 1):
                    copy.wait()

        @pl.when(running & (block == 0) & (part < half))
        def _():
            @pl.when(part == tiles - 1)
            def _():
                for s in range(3):
                    fill(3 * part + s)

            for s in range(3):
                load_feed(3 * part + s, s).wait()

        @pl.when(running & (part < half))
        def _():
            at = pl.ds(pl.multiple_of(part * wide, wide), wide)
            gate = dot_nn(xs[slot], wg[:, at])
            up = dot_nn(xs[slot], wu[:, at])
            back_value = dot_nn(ogs[slot], wd[:, at])
            sig = jax.nn.sigmoid(gate)
            act = gate * sig
            hs[:, at] = (act * up).astype(BF)
            gs[:, at] = (back_value * up * sig * (1.0 + gate * (1.0 - sig))).astype(BF)
            us[:, at] = (back_value * act).astype(BF)

            @pl.when(block == 0)
            def _():
                def spread_out(o, carry):
                    to = rows_of(o, wide)
                    add = dot_nt(gs[:, at], wg[to, at]) + dot_nt(us[:, at], wu[to, at])

                    @pl.when(part == 0)
                    def _():
                        early_sum[o] = add

                    @pl.when(part > 0)
                    def _():
                        early_sum[o] = early_sum[o] + add

                    return carry

                lax.fori_loop(0, acc.shape[1] // wide, spread_out, 0)

        @pl.when(running & (part == half - 1))
        def _():
            tree.settle((block + held) * per_block, per_block)

            @pl.when(block == 0)
            def _():
                for o in range(acc.shape[1] // wide):
                    acc[pl.ds(0, BLOCK_ROWS), pl.ds(o * wide, wide)] = early_sum[o].astype(BF)
                tree.send_block(blocks)

        @pl.when(running & (part >= half))
        def _():
            at = pl.ds(pl.multiple_of((part - half) * wide, wide), wide)

            @pl.when(block > 0)
            def _():
                acc[rows_of(block % held, BLOCK_ROWS), at] = (
                    dot_nt(gs[...], wg[at, :]) + dot_nt(us[...], wu[at, :])
                ).astype(BF)

            ps[:, at] = dot_nt(hs[...], wd[at, :]).astype(BF)

        @pl.when(running & (part == per_block - 1))
        def _():
            for copy in store_block(block):
                copy.start()

            @pl.when(block + 2 < blocks)
            def _():
                for copy in load_block(block + 2):
                    copy.start()

            @pl.when(block > 0)
            def _():
                tree.send_block(blocks + block)

        late = i - turn_at

        @pl.when(late == 0)
        def _():
            for copy in store_block(blocks - 1):
                copy.wait()
            lax.fori_loop(4, 4 + feeds, leave, 0)
            for m in range(4):
                gather.settle(m)
            for p in range(pairs):
                cross(p, 0).wait_send()
                cross(p, 1).wait_send()
            scatter.ready()
            pl.semaphore_signal(ready_x, inc=1, device_id=plane.x_next, device_id_type=MESH)
            pl.semaphore_signal(ready_y, inc=1, device_id=plane.y_next, device_id_type=MESH)
            first_rows = pl.ds(0, shard_len)
            first = pltpu.make_async_copy(
                lefts[2].at[first_rows], wg.at[pl.ds(rows, shard_len)], lhs_sem.at[1]
            )
            first.start()
            out_weight.start()
            left_copy(0).start()
            right_copy(0, 0).start()
            right_copy(1, 0).start()
            first.wait()
            out_weight.wait()
            group_grads(0)
            pl.semaphore_wait(ready_x, 1)
            pl.semaphore_wait(ready_y, 1)

        later = late - 3

        @pl.when((later >= 0) & (later % per_block == 0) & (later < per_sum))
        def _():
            block = later // per_block
            tree.settle((2 * blocks - held + block) * per_block, per_block)
            load_part(block).start()
            load_part(block).wait()
            tree.send_block(2 * blocks + block)

        @pl.when((later >= per_sum) & (later % per_block == 0) & (later < 2 * per_sum))
        def _():
            block = later // per_block - blocks
            tree.settle((3 * blocks - held + block) * per_block, per_block)
            half = acc.shape[1] // 2
            for s in range(2):
                at = pl.ds(s * half, half)
                acc[rows_of(block % held, BLOCK_ROWS), at] = dot_nt(
                    dqkv[rows_of(block, BLOCK_ROWS)], wu[at, pl.ds(0, 3 * wide)]
                ).astype(BF)
            tree.send_block(3 * blocks + block)

        @pl.when((late >= 1) & (late < 1 + 3 * heads) & ((late - 1) % 3 == 0))
        def _():
            pair_back((late - 1) // 3)

        second_at = 3 + per_block + 1

        @pl.when(late == second_at)
        def _():
            @pl.when(tree.is_mid)
            def _():
                gm_drop.finish()
                tok_feed.begin()

            second = pltpu.make_async_copy(
                lefts[2].at[pl.ds(shard_len, rows - shard_len)],
                wg.at[pl.ds(rows + shard_len, rows - shard_len)],
                lhs_sem.at[1],
            )
            second.start()
            second.wait()
            for group in range(1, groups):
                group_grads(group)
            left_copy(1).start()
            head_weights.start()

        more = late - second_at - 1

        @pl.when((more >= 0) & (more < 3 * (pairs - heads)) & (more % 3 == 0))
        def _():
            pair_back(heads + more // 3)

        join = late - second_at - 1 - 3 * (pairs - heads) - 1

        @pl.when((join >= 0) & (join < pairs // 2))
        def _():
            pair_join(2 * join)
            pair_join(2 * join + 1)

        @pl.when(join == pairs // 2)
        def _():
            head_weights.wait()

        tick = late - 21

        @pl.when((tick >= 0) & (tick % 3 == 0))
        def _():
            k = tick // 3
            scatter.join_cores(k - 1)
            scatter.join_diagonal(k - 2)

            @pl.when(k < columns)
            def _():
                right_arrived(k)

            for p in range(4):
                @pl.when(k == starts[p])
                def _():
                    left_copy(p).wait()

            scatter.compute(k)
            for p in (2, 3):
                @pl.when(k == starts[p - 1] - 1)
                def _():
                    left_copy(p).start()

            right_start(k + 2)
            scatter.finish(k - 3)

        return carry

    steps = max(count + lag + 2, turn_at + 21 + 3 * (columns + 2) + 1)
    lax.fori_loop(0, steps, step, 0)
    scatter.drain()
    tree.drain()


def layer(tokens, shards, out_grad, block_ids, cosine, sine, groups):
    rows, model = tokens.shape
    width, hidden = shards[0].shape[1], shards[-1].shape[1]
    heads = width // HD
    pairs = groups * heads
    shard_len = rows // groups
    count = 4 * rows // CHUNK
    total = sum(shard.shape[1] for shard in shards)
    chunks = total // width
    sem = lambda *shape: pltpu.SemaphoreType.DMA(shape)
    shape = jax.ShapeDtypeStruct
    slots = lambda kind: [pltpu.VMEM((2, CHUNK, model), kind), sem(2)]
    block = lambda *lead: pltpu.VMEM((*lead, BLOCK_ROWS, model), BF)
    outs = pl.pallas_call(
        functools.partial(layer_kernel, CHUNK, count, groups, heads),
        out_shape=(
            shape((model, total), BF),
            shape((rows, model), BF),
            shape((4 * rows, model), BF),
            shape((rows, model), F32),
            shape((rows, model), F32),
            shape((rows, hidden), BF),
            shape((rows, 2 * hidden), BF),
            shape((rows, model), BF),
            shape((BLOCK_ROWS, total), F32),
        ),
        in_specs=[ANY] * 9 + [VMEM] + [ANY] * 2,
        out_specs=(ANY,) * 9,
        scratch_shapes=tree_scratch(CHUNK, 2 * BLOCK_ROWS, model)
        + slots(F32) + slots(BF) + slots(F32) + slots(BF) + [sem(2)]
        + [pltpu.VMEM((model, hidden), BF) for _ in range(3)]
        + [sem(3 * hidden // width), block(2), block(2), sem(2, 2), block(4), sem(4)]
        + [
            sem(rows // BLOCK_ROWS), sem(2), pltpu.VMEM((BLOCK_ROWS, total), BF), sem(8),
            pltpu.VMEM((pairs, shard_len, HD), BF),
            pltpu.VMEM((pairs, shard_len, 2 * HD), BF),
            pltpu.VMEM((pairs, shard_len, 2 * HD), BF),
            pltpu.VMEM((rows, width), BF),
            pltpu.VMEM((pairs, 1, shard_len), F32),
            sem(2, pairs), sem(2, pairs), sem(8, chunks), sem(8, chunks),
            sem(2), sem(2), sem(pairs), sem(pairs), pltpu.SemaphoreType.REGULAR, pltpu.SemaphoreType.REGULAR,
            pltpu.VMEM((groups, 8, shard_len), F32),
            pltpu.VMEM((2, groups, shard_len, HD), BF),
            pltpu.VMEM((shard_len, HD), F32),
            pltpu.VMEM((shard_len, HD), F32),
            sem(2),
        ]
        + scatter_scratch(BLOCK_ROWS, width),
        compiler_params=params(1),
    )(tokens, *shards, out_grad, block_ids, cosine, sine)
    return outs[2], outs[-1]


def tree_body(
    tokens,
    block_ids,
    query_weight,
    key_weight,
    value_weight,
    out_weight,
    gate_weight,
    up_weight,
    down_weight,
    out_grad,
):
    groups, shard_len, model = tokens.shape
    rows = groups * shard_len
    width, hidden = query_weight.shape[1], gate_weight.shape[1]
    ranks = lax.axis_size("seq")
    frequency = np.exp(np.arange(HD // 2) * (-2.0 * math.log(THETA) / HD))
    angles = np.arange(ranks * shard_len)[:, None] * frequency[None, :]
    table = lambda *halves: jnp.asarray(
        np.concatenate(halves, axis=1).reshape(ranks, shard_len, HD).astype(np.float32)
    )
    cosine = table(np.cos(angles), np.cos(angles))
    sine = table(-np.sin(angles), np.sin(angles))
    flat_tokens = tokens.reshape(rows, model)
    grad_low = out_grad.reshape(rows, model)
    shards = (query_weight, key_weight, value_weight, out_weight, gate_weight, up_weight, down_weight)
    results, grads = layer(
        flat_tokens, shards, grad_low, block_ids, cosine, sine, groups
    )
    at = 3 * hidden + width
    return (
        results[2 * rows : 3 * rows].reshape(tokens.shape),
        results[3 * rows :].reshape(tokens.shape),
        grads[:, at : at + width],
        grads[:, at + width : at + 2 * width],
        grads[:, at + 2 * width :],
        grads[:, 3 * hidden : at],
        grads[:, :hidden],
        grads[:, hidden : 2 * hidden],
        grads[:, 2 * hidden : 3 * hidden],
    )


def solution(mesh):
    in_specs = (
        P("dp", "seq", None),
        P("dp", None),
        P(("dp", "seq"), "mp"),
        P(("dp", "seq"), "mp"),
        P(("dp", "seq"), "mp"),
        P(("dp", "seq"), "mp"),
        P(("dp", "seq"), "mp"),
        P(("dp", "seq"), "mp"),
        P(("dp", "seq"), "mp"),
        P("dp", "seq", None),
    )
    out_specs = (
        P("dp", "seq", None),
        P("dp", "seq", None),
        P(("dp", "seq"), "mp"),
        P(("dp", "seq"), "mp"),
        P(("dp", "seq"), "mp"),
        P(("dp", "seq"), "mp"),
        P(("dp", "seq"), "mp"),
        P(("dp", "seq"), "mp"),
        P(("dp", "seq"), "mp"),
    )
    fits = mesh.shape["dp"] == 4 and mesh.shape["seq"] == 2 and mesh.shape["mp"] == 4
    body = tree_body if fits else general_body
    return jax.shard_map(body, mesh=mesh, in_specs=in_specs, out_specs=out_specs, check_vma=False)
```
